32 devices in a mesh: fold: 2 (over x), row: 8 (over z, y), leaf: 2 (over core).
Axes of the slice: x: 2, y: 2, z: 4, core: 2. Of those that a mesh axis runs over, the one named last changes fastest.
Arguments:
- features: bfloat16 [64, 262144], P(None, ('fold', 'row', 'leaf')), parts along dimension 1, may hold values from -6 to 6
- hessian: float32 [262144], P(('fold', 'row', 'leaf')), parts along dimension 0, as said below
- gradient: float32 [262144], P(('fold', 'row', 'leaf')), parts along dimension 0, may hold values from -6 to 6
- leaf_index: int32 [262144, 1], P(('fold', 'row', 'leaf')), parts along dimension 0, may hold values from 0 to 255; in each aligned block of 8192 rows (0 to 8191, 8192 to 16383, ...) at most 64 rows name the same one
- train_range: int32 [4], P('fold'), parts along dimension 0, may hold values from 0 to 131072, as said below
Outputs:
- coefficients: float32 [512, 65], P('fold'), parts along dimension 0
- next_gradient: float32 [262144], P(('fold', 'row', 'leaf')), parts along dimension 0
The draws below stay inside these ranges and needn't reach their ends.
There are 2 independent parts, one for each index of `fold`. The reference program is written for one: setup_inputs(seed, part) draws one part's arguments, and reference() takes and returns one part's arrays. A program takes and returns all parts, laid end to end along the dimension named above; each array names one. Nothing has to cross between parts.
Inputs may be any that keep to these rules, and one draw needn't show every extreme that they name: train_range[0] < 32768 and train_range[1] >= 98304. `hessian`: positive. `leaf_index`: among the 8192 rows of one device, no leaf holds more than 64 rows, and some leaf holds exactly 64.
All inputs are finite; a program needn't handle non-finite values.
Results may differ from the reference program's by a relative error of at most 0.0031.
Values may be sent and summed in bfloat16 or wider, within the bound.
No kernel may reach another device: no remote copies, remote signals or barrier semaphores. Data moves between devices by JAX's collectives and lax.ppermute only.
A program may use at most 64 MiB of HBM per device.

```python
import math
import jax
import jax.numpy as jnp
import numpy as np
from jax import lax

REGRESSORS = 64
LEAVES = 256
ROWS_DEV = 8192
ROWS = 131072


def draw_hessian(key, part):
    key = jax.random.fold_in(key, 11)
    position = jnp.arange(ROWS, dtype=jnp.float32) / ROWS
    rising = 1.0 + 2.0 * position
    base = jnp.exp(jax.random.uniform(key, (ROWS,), jnp.float32, jnp.log(0.2), jnp.log(2.0)))
    return base * rising


def draw_train_range(key, part):
    key = jax.random.fold_in(key, 23)
    first_key, end_key = jax.random.split(key)
    first_row = jax.random.randint(first_key, (1,), 0, ROWS // 4)
    end_row = jax.random.randint(end_key, (1,), 3 * ROWS // 4, ROWS + 1)
    return jnp.concatenate([first_row, end_row]).astype(jnp.int32)


def block_scale(own_key, shape, shards, least, top_value):
    def one(dim, parts):
        heights = jax.random.uniform(jax.random.fold_in(jax.random.fold_in(own_key, 6), dim), (parts,), jnp.float32, least / len(shards), top_value / len(shards))
        return jnp.repeat(jnp.exp(heights), shape[dim] // parts).reshape((-1,) + (1,) * (len(shape) - dim - 1))

    factor_of = one(*shards[0])
    for cut in shards[1:]:
        factor_of = factor_of * one(*cut)
    return factor_of


def assign_block(own_key, own, number, rows, number_of, top, most, lean):
    sequence = jax.random.permutation(own_key, number_of)
    packed, usual = shares(number_of, rows * top, most, lean, True), shares(number_of, rows * top, most, lean, False)
    places = jnp.arange(number_of)

    def named(sizes, rotation):
        used = int((sizes > 0).sum())
        fixed = max(1, used // 4)
        passed = fixed + (places - fixed + rotation * (used - fixed)) % max(1, number_of - fixed)
        return jnp.zeros((number_of,), jnp.int32).at[sequence[jnp.where(places < fixed, places, passed)]].set(jnp.asarray(sizes, jnp.int32))

    sizes = jnp.where(number % 4 == 0, named(packed, number // 4), named(usual, number - number // 4 - 1))
    mixed = jax.random.permutation(jax.random.fold_in(own, 3), number_of)
    giver, taker = mixed[0:number_of // 2 * 2:2], mixed[1:number_of // 2 * 2:2]
    margin = jnp.minimum(sizes[giver] - 1, most - sizes[taker]) // 2
    margin = jnp.where((giver == sequence[0]) | (taker == sequence[0]) | (sizes[taker] == 0), 0, jnp.maximum(margin, 0))
    passed = jax.random.randint(jax.random.fold_in(own, 4), (number_of // 2,), 0, 1 << 20) % (margin + 1)
    sizes = sizes.at[giver].add(-passed).at[taker].add(passed)
    labels = jnp.searchsorted(jnp.cumsum(sizes), jnp.arange(rows * top), side="right").astype(jnp.int32)
    table = labels.reshape(top, rows).T
    table = table[jax.random.permutation(jax.random.fold_in(own, 1), rows)]
    rotation = jax.random.randint(jax.random.fold_in(own, 2), (rows, 1), 0, top)
    return jnp.take_along_axis(table, (jnp.arange(top)[None, :] + rotation) % top, axis=1)


def shares(count, total, most, slope, full):
    loads = [(1 << 20) // math.isqrt(grade ** slope) + 1 for grade in range(1, count + 1)]
    largest = most if full else min(most, max(-(-total // count), total * loads[0] // sum(loads)))
    least = 1 if total - largest >= count - 1 else 0
    holding, spare = [largest] + [least] * (count - 1), total - largest - least * (count - 1)
    while spare > 0:
        free = [i for i in range(1, count) if holding[i] < largest] or [i for i in range(1, count) if holding[i] < most]
        mass, left = sum([loads[i] for i in free]), spare
        for i in free:
            addition = min(most - holding[i], max(1, left * loads[i] // mass), spare)
            holding[i] = holding[i] + addition
            spare = spare - addition
    return np.array(holding)


def scatter_about(own_key, dims, spread, reach, cuts=(), kind=jnp.bfloat16):
    level = block_scale(own_key, dims, cuts, -0.22, 0.18) if cuts else 1.0
    result = jax.random.normal(own_key, dims, jnp.float32) * spread * level
    return jnp.minimum(jnp.maximum(result, -reach), reach).astype(kind)


def setup_inputs(seed: int = 0, part: int = 0) -> dict:
    keys = jax.random.split(jax.random.key(seed), 6)
    part_keys = jax.random.split(jax.random.fold_in(keys[5], part), 6)
    features = scatter_about(part_keys[0], (REGRESSORS, ROWS), 1.0, 6.0, ((1, 16),))
    hessian = draw_hessian(jax.random.fold_in(jax.random.fold_in(keys[5], part), 71), part)
    gradient = scatter_about(part_keys[2], (ROWS,), 1.0, 6.0, ((0, 16),), jnp.float32)
    leaf_index_keys = jax.random.split(jax.random.fold_in(part_keys[3], 1), ROWS // ROWS_DEV)
    leaf_index_turns = jax.random.permutation(jax.random.fold_in(part_keys[3], 3), ROWS // ROWS_DEV)
    leaf_index = jax.vmap(lambda own, number: assign_block(jax.random.fold_in(part_keys[3], 2), own, number, ROWS_DEV, LEAVES, 1, 2 * ROWS_DEV // LEAVES, 1))(leaf_index_keys, leaf_index_turns).reshape((ROWS, 1))
    train_range = draw_train_range(jax.random.fold_in(jax.random.fold_in(keys[5], part), 71), part)
    return {"features": features, "hessian": hessian, "gradient": gradient, "leaf_index": leaf_index, "train_range": train_range}


def solve_leaves(normal_sums, ridge):
    width = normal_sums.shape[2]
    square = normal_sums[:, :width, :]
    system = 0.5 * (square + jnp.swapaxes(square, 1, 2)) + ridge * jnp.eye(width, dtype=jnp.float32)[None]
    factor = jnp.linalg.cholesky(system)
    target = -normal_sums[:, width, :][:, :, None]
    middle = jax.scipy.linalg.solve_triangular(factor, target, lower=True)
    return jax.scipy.linalg.solve_triangular(factor, middle, lower=True, trans=1)[:, :, 0]

def reference(features, hessian, gradient, leaf_index, train_range):
    leaf = leaf_index[:, 0].astype(jnp.int32)
    position = jnp.arange(ROWS, dtype=jnp.int32)
    inside = ((position >= train_range[0]) & (position < train_range[1])).astype(jnp.float32)
    design = jnp.concatenate([features, jnp.ones((1, ROWS), jnp.bfloat16)], 0)
    design_f = design.astype(jnp.float32)
    weighted = jnp.concatenate([(inside * hessian)[None] * design_f, (inside * gradient)[None]], 0).astype(jnp.bfloat16)
    piece = math.gcd(ROWS, 1024)
    blocks = ROWS // piece
    weighted_b = weighted.astype(jnp.float32).reshape(REGRESSORS + 2, blocks, piece).transpose(1, 0, 2)
    design_b = design_f.reshape(REGRESSORS + 1, blocks, piece).transpose(1, 0, 2)
    leaf_b = leaf.reshape(blocks, piece)

    def accumulate(total, pieces):
        wpart, dpart, lpart = pieces
        outer = wpart.T[:, :, None] * dpart.T[:, None, :]
        return (total + jax.ops.segment_sum(outer, lpart, num_segments=LEAVES), None)
    start = jnp.zeros((LEAVES, REGRESSORS + 2, REGRESSORS + 1), jnp.float32)
    normal_sums, _ = lax.scan(accumulate, start, (weighted_b, design_b, leaf_b))
    hess_total = jnp.sum(weighted[REGRESSORS].astype(jnp.float32))
    ridge = 0.5 * hess_total / LEAVES
    coefficients = solve_leaves(normal_sums, ridge)
    picked = jnp.take(coefficients.T, leaf, axis=1)
    predicted = jnp.sum(picked * design_f, 0)
    return (coefficients, gradient + hessian * predicted)
```

```python
import functools
import jax
import jax.numpy as jnp
from jax import lax
from jax.experimental import pallas as pl
from jax.experimental.pallas import tpu as pltpu
from jax.sharding import PartitionSpec as P

LEAVES = 256
STEP = 2048
APPLY_STEP = 2048
CUTS = ((0, 3), (3, 6), (6, 10))
SCATTER_BITS = (1, 2)
F32, BF16, I32 = jnp.float32, jnp.bfloat16, jnp.int32
NT = (((1,), (1,)), ((), ()))


def pair_layout(regress):
    subs, first = [], {}
    for a in range(0, regress, 2):
        blocks = a // 8 + 1
        for one in (a, a + 1):
            for m in range(blocks // 2):
                first[one, 2 * m] = 16 * len(subs)
                first[one, 2 * m + 1] = 16 * len(subs) + 8
                subs.append(("full", one, m))
        if blocks % 2:
            first[a, blocks - 1] = 16 * len(subs)
            first[a + 1, blocks - 1] = 16 * len(subs) + 8
            subs.append(("half", a, blocks - 1))
    return subs, first


def sums_kernel(subs, out_width, step, with_total, me_ref, range_ref, feat_ref, hess_ref, grad_ref, leaf_ref, keep_ref, send_ref, w_ref, total_ref):
    k = pl.program_id(0)
    regress = feat_ref.shape[0]

    @pl.when(k == 0)
    def _():
        keep_ref[...] = jnp.zeros_like(keep_ref)
        send_ref[...] = jnp.zeros_like(send_ref)
        total_ref[...] = jnp.zeros_like(total_ref)

    position = me_ref[1] + k * step + lax.broadcasted_iota(I32, (1, step), 1)
    inside = jnp.where((position >= range_ref[0]) & (position < range_ref[1]), 1.0, 0.0)
    hess = hess_ref[...] * inside
    grad = (grad_ref[...] * inside).astype(BF16)
    hess_b = hess.astype(BF16)
    leaf = leaf_ref[...] ^ me_ref[0]
    hot = jnp.where(lax.broadcasted_iota(I32, (LEAVES, step), 0) == leaf, 1.0, 0.0).astype(BF16)
    feat = feat_ref[...]
    feat_f = feat.astype(F32)
    w_ref[...] = feat_f * hess

    @functools.lru_cache(None)
    def weight(a, rows):
        return jnp.broadcast_to(w_ref[a:a + 1, :], (rows, step))

    @functools.lru_cache(None)
    def weight_b(a):
        return weight(a, 16).astype(BF16)

    @functools.lru_cache(None)
    def twice(m):
        part = feat_f[8 * m:8 * m + 8]
        return jnp.concatenate([part, part], 0).astype(BF16)

    def rows_of(sub):
        kind, a, m = sub
        if kind == "full":
            return weight_b(a) * feat[16 * m:16 * m + 16]
        if kind == "half":
            both = jnp.concatenate([weight(a, 8), weight(a + 1, 8)], 0).astype(BF16)
            tile = both * twice(m)
            if a == 0:
                row = lax.broadcasted_iota(I32, (16, step), 0)
                tile_f = tile.astype(F32)
                tile_f = jnp.where(row == 1, hess_b.astype(F32), tile_f)
                tile_f = jnp.where(row == 2, grad.astype(F32), tile_f)
                tile = tile_f.astype(BF16)
            return tile
        if kind == "weight":
            return w_ref[16 * m:16 * m + 16, :].astype(BF16)
        if kind == "zero":
            return jnp.zeros((16, step), BF16)
        exact = feat_f[16 * m:16 * m + 16] * grad.astype(F32)
        high = exact.astype(BF16)
        if kind == "grad_high":
            return high
        return (exact - high.astype(F32)).astype(BF16)

    tiles = len(subs) * 16 // 256
    for t in range(tiles):
        rows = jnp.concatenate([rows_of(s) for s in subs[16 * t:16 * t + 16]], 0)
        part = lax.dot_general(hot, rows, NT, preferred_element_type=F32)
        if (t + 1) * 256 > out_width:
            part = part[:, :128] + part[:, 128:]
        lanes = slice(t * 256, t * 256 + part.shape[1])
        keep_ref[:, lanes] += part[:LEAVES // 2]
        send_ref[:, lanes] += part[LEAVES // 2:]
    if with_total:
        total_ref[...] += hess_b.astype(F32)

        @pl.when(k == pl.num_programs(0) - 1)
        def _():
            total = jnp.sum(total_ref[...])
            lane = lax.broadcasted_iota(I32, (LEAVES // 2, 128), 1)
            for half_ref in (keep_ref, send_ref):
                half_ref[:, :128] = jnp.where(lane == 3, total, half_ref[:, :128])


def sums_call(subs, out_width, step, with_total, me, train_range, features, hessian, gradient, leaf):
    regress, rows = features.shape
    return pl.pallas_call(
        functools.partial(sums_kernel, subs, out_width, step, with_total),
        grid=(rows // step,),
        in_specs=[
            pl.BlockSpec(memory_space=pltpu.SMEM),
            pl.BlockSpec(memory_space=pltpu.SMEM),
            pl.BlockSpec((regress, step), lambda k: (0, k)),
            pl.BlockSpec((1, step), lambda k: (0, k)),
            pl.BlockSpec((1, step), lambda k: (0, k)),
            pl.BlockSpec((1, step), lambda k: (0, k)),
        ],
        out_specs=[pl.BlockSpec((LEAVES // 2, out_width), lambda k: (0, 0))] * 2,
        out_shape=[jax.ShapeDtypeStruct((LEAVES // 2, out_width), F32)] * 2,
        scratch_shapes=[pltpu.VMEM((regress, step), F32), pltpu.VMEM((1, step), F32)],
        compiler_params=pltpu.CompilerParams(vmem_limit_bytes=48 << 20),
        cost_estimate=pl.CostEstimate(flops=2 * LEAVES * rows * len(subs) * 16, bytes_accessed=rows * 144 + LEAVES * out_width * 4, transcendentals=0),
    )(me, train_range, features, hessian, gradient, leaf)


def solve_kernel(regress, first, starts, parts, *refs):
    chunks = len(starts)
    in_refs, (out_ref, t_ref, u_ref, z_ref, c_ref) = refs[:chunks * parts], refs[chunks * parts:]
    held = in_refs[0].shape[0]
    for c, start in enumerate(starts):
        group = in_refs[c * parts:(c + 1) * parts]
        for lane in range(0, group[0].shape[1], 128):
            tile = group[0][:, lane:lane + 128]
            for ref in group[1:]:
                tile = tile + ref[:, lane:lane + 128]
            tile = jnp.concatenate([tile, jnp.zeros((128 - held, 128), F32)], 0)
            t_ref[start + lane:start + lane + 128, :] = tile.T
    last = regress
    first = dict(first)
    for m in range(regress // 8):
        first[last, m] = starts_of_last(regress) + 8 * m
    grad_at = starts_of_last(regress) + regress
    corner = t_ref[first[0, 0]:first[0, 0] + 8, :]
    real = lax.broadcasted_iota(I32, (1, 128), 1) < held
    ridge = jnp.where(real, corner[3:4] * (0.5 / LEAVES), 1.0)
    blocks = regress // 8

    def row(a, m):
        return t_ref[first[a, m]:first[a, m] + 8, :]

    def pivot(a, own, count):
        inverse = 1.0 / (own + ridge)
        for m in range(count):
            u_ref[a, 8 * m:8 * m + 8, :] = row(a, m) * inverse
        return inverse

    def reduce_target(a, inverse, value):
        scaled = value * inverse
        z_ref[a:a + 1, :] = scaled
        for m in range((a + 7) // 8):
            t_ref[grad_at + 8 * m:grad_at + 8 * m + 8, :] -= row(a, m) * scaled

    for m in range(blocks):
        t_ref[grad_at + 8 * m:grad_at + 8 * m + 8, :] = -t_ref[grad_at + 8 * m:grad_at + 8 * m + 8, :]
    inverse = pivot(last, corner[1:2], blocks)
    reduce_target(last, inverse, -corner[2:3])
    for q in range(blocks - 1, -1, -1):
        for top in (8 * q + 4, 8 * q):
            some = range(top + 3, top - 1, -1)
            total = {(a, m): row(a, m) for a in some for m in range(q + 1)}
            for k in range(last, 8 * q + 7, -1):
                line = [row(k, m) for m in range(q + 1)]
                for a in some:
                    scale = u_ref[k, a:a + 1, :]
                    for m in range(q + 1):
                        total[a, m] = total[a, m] - scale * line[m]
            for (a, m), value in total.items():
                t_ref[first[a, m]:first[a, m] + 8, :] = value
        for a in range(8 * q + 7, 8 * q - 1, -1):
            total = [row(a, m) for m in range(q + 1)]
            for k in range(8 * q + 7, a, -1):
                scale = u_ref[k, a:a + 1, :]
                for m in range(q + 1):
                    total[m] = total[m] - scale * row(k, m)
            for m in range(q + 1):
                t_ref[first[a, m]:first[a, m] + 8, :] = total[m]
            at = first[a, q] + a % 8
            inverse = pivot(a, t_ref[at:at + 1, :], q + 1)
            reduce_target(a, inverse, t_ref[grad_at + a:grad_at + a + 1, :])
    c_ref[...] = jnp.zeros_like(c_ref)
    for q in range(blocks + 1):
        rows = range(8 * q, min(8 * q + 8, regress + 1))
        known = {}
        for k in rows:
            value = z_ref[k:k + 1, :]
            if q:
                products = u_ref[k, 0:8, :] * c_ref[0:8, :]
                for m in range(1, q):
                    products = products + u_ref[k, 8 * m:8 * m + 8, :] * c_ref[8 * m:8 * m + 8, :]
                value = value - jnp.sum(products, 0, keepdims=True)
            known[k] = value
        for k in rows:
            for b in range(8 * q, k):
                known[k] = known[k] - u_ref[k, b:b + 1, :] * known[b]
        for k in rows:
            c_ref[k:k + 1, :] = known[k]
    out_ref[...] = c_ref[...].T[:held]


def starts_of_last(regress):
    return 16 * len(pair_layout(regress)[0])


def solve_call(regress, starts, pieces):
    parts, held = len(pieces[0]), pieces[0][0].shape[0]
    lanes = sum(group[0].shape[1] for group in pieces)
    return pl.pallas_call(
        functools.partial(solve_kernel, regress, pair_layout(regress)[1], starts, parts),
        out_shape=jax.ShapeDtypeStruct((held, 128), F32),
        in_specs=[pl.BlockSpec(memory_space=pltpu.VMEM)] * (parts * len(pieces)),
        out_specs=pl.BlockSpec(memory_space=pltpu.VMEM),
        scratch_shapes=[
            pltpu.VMEM((lanes, 128), F32),
            pltpu.VMEM((regress + 1, regress, 128), F32),
            pltpu.VMEM((72, 128), F32),
            pltpu.VMEM((128, 128), F32),
        ],
        compiler_params=pltpu.CompilerParams(vmem_limit_bytes=32 << 20),
    )(*[part for group in pieces for part in group])


def apply_kernel(places, block, width, step, me_ref, *refs):
    part_refs = refs[:len(places)]
    feat_ref, hess_ref, grad_ref, leaf_ref, coef_ref, next_ref, rel_ref, high_ref, low_ref = refs[len(places):]
    k = pl.program_id(0)
    regress = feat_ref.shape[0]

    @pl.when(k == 0)
    def _():
        for ref, owners in zip(part_refs, places):
            for at, place in enumerate(owners):
                rel_ref[place * block:(place + 1) * block, :] = ref[at * block:(at + 1) * block, :]
        def put(i, carry):
            origin = pl.multiple_of(i * block, block)
            target = pl.multiple_of(origin ^ me_ref[0], block)
            coef_ref[pl.ds(target, block), :] = rel_ref[pl.ds(origin, block), :][:, :width]
            return carry
        lax.fori_loop(0, LEAVES // block, put, 0)
        turned = rel_ref[...].T[:high_ref.shape[0]]
        high = turned.astype(BF16)
        high_ref[...] = high
        low_ref[...] = (turned - high.astype(F32)).astype(BF16)

    leaf = leaf_ref[...] ^ me_ref[0]
    hot = jnp.where(lax.broadcasted_iota(I32, (LEAVES, step), 0) == leaf, 1.0, 0.0).astype(BF16)
    picked = jnp.dot(high_ref[...], hot, preferred_element_type=F32) + jnp.dot(low_ref[...], hot, preferred_element_type=F32)
    feat = feat_ref[...].astype(F32)
    predicted = jnp.sum(picked[:regress] * feat, 0, keepdims=True) + picked[regress:regress + 1]
    next_ref[...] = grad_ref[...] + hess_ref[...] * predicted


def apply_call(places, block, parts, step, me, features, hessian, gradient, leaf):
    regress, rows = features.shape
    width = regress + 1
    return pl.pallas_call(
        functools.partial(apply_kernel, places, block, width, step),
        grid=(rows // step,),
        in_specs=[pl.BlockSpec(memory_space=pltpu.SMEM)]
        + [pl.BlockSpec(part.shape, lambda k: (0, 0)) for part in parts]
        + [
            pl.BlockSpec((regress, step), lambda k: (0, k)),
            pl.BlockSpec((1, step), lambda k: (0, k)),
            pl.BlockSpec((1, step), lambda k: (0, k)),
            pl.BlockSpec((1, step), lambda k: (0, k)),
        ],
        out_specs=[pl.BlockSpec((LEAVES, width), lambda k: (0, 0)), pl.BlockSpec((1, step), lambda k: (0, k))],
        out_shape=[jax.ShapeDtypeStruct((LEAVES, width), F32), jax.ShapeDtypeStruct((1, rows), F32)],
        scratch_shapes=[pltpu.VMEM((LEAVES, 128), F32), pltpu.VMEM((80, LEAVES), BF16), pltpu.VMEM((80, LEAVES), BF16)],
        compiler_params=pltpu.CompilerParams(vmem_limit_bytes=32 << 20),
    )(me, *parts, features, hessian, gradient, leaf)


def row_groups(rows, sizes):
    groups, shift = [], 0
    while (1 << shift) < rows:
        bits = min(sizes[min(len(groups), len(sizes) - 1)], (rows - 1).bit_length() - shift)
        groups.append((shift, bits))
        shift += bits
    return groups


def swap_rows(x, rows, distance):
    return lax.ppermute(x, "row", [(r, r ^ distance) for r in range(rows)])


def body(features, hessian, gradient, leaf_index, train_range):
    regress, local = features.shape
    rows = lax.axis_size("row")
    block = LEAVES // (2 * rows)
    groups = row_groups(rows, SCATTER_BITS)
    row, core = lax.axis_index("row"), lax.axis_index("leaf")

    def place_of(core, row):
        place = core
        for shift, bits in groups:
            place = (place << bits) | ((row >> shift) & ((1 << bits) - 1))
        return place

    me = jnp.stack([place_of(core, row) * block, (row * 2 + core) * local]).astype(I32)
    rowed = [hessian.reshape(1, local), gradient.reshape(1, local), leaf_index.reshape(1, local)]
    subs, first = pair_layout(regress)
    count = regress // 16
    subs = subs + [("weight", 0, m) for m in range(count)] + [("grad_high", 0, m) for m in range(count)]
    subs = subs + [("zero", 0, 0)] * count + [("grad_low", 0, m) for m in range(count)]
    pieces, starts = [], []
    for c, (begin, end) in enumerate(CUTS):
        part = subs[16 * begin:16 * end]
        out_width = 256 * (end - begin) - (128 if end * 16 == len(subs) else 0)
        keep, send = sums_call(part, out_width, STEP, c == 0, me, train_range, features, *rowed)
        got = [lax.ppermute(send, "leaf", [(0, 1), (1, 0)])]
        mine = [keep]
        size = LEAVES // 2
        for shift, bits in groups:
            size >>= bits
            cut = [sum([x[d * size:(d + 1) * size] for x in mine + got][1:], mine[0][d * size:(d + 1) * size]) for d in range(1 << bits)]
            mine = cut[:1]
            got = [swap_rows(cut[d], rows, d << shift) for d in range(1, 1 << bits)]
        group = mine + got
        if block % 8:
            group = [jnp.pad(x, ((0, -block % 8), (0, 0))) for x in group]
        pieces.append(group)
        starts.append(256 * begin)
    coef = solve_call(regress, starts, pieces)[:block]
    both = jnp.concatenate([coef, lax.ppermute(coef, "leaf", [(0, 1), (1, 0)])], 0)
    held = [([0], both)]
    for shift, bits in row_groups(rows, [3]):
        names = [d for owners, _ in held for d in owners]
        array = jnp.concatenate([x for _, x in held], 0) if len(held) > 1 else held[0][1]
        held = held + [([n ^ (d << shift) for n in names], swap_rows(array, rows, d << shift)) for d in range(1, 1 << bits)]
    places = [[place_of(c, d) for d in owners for c in range(2)] for owners, _ in held]
    coefficients, following = apply_call(places, block, [x for _, x in held], APPLY_STEP, me, features, *rowed)
    return coefficients, following.reshape(local)


def solution(mesh):
    placed = (
        P(None, ("fold", "row", "leaf")),
        P(("fold", "row", "leaf")),
        P(("fold", "row", "leaf")),
        P(("fold", "row", "leaf"), None),
        P("fold"),
    )
    return jax.shard_map(
        body,
        mesh=mesh,
        in_specs=placed,
        out_specs=(P("fold", None), P(("fold", "row", "leaf"))),
        check_vma=False,
    )
```

```python
import functools
import jax
import jax.numpy as jnp
from jax import lax
from jax.experimental import pallas as pl
from jax.experimental.pallas import tpu as pltpu
from jax.sharding import PartitionSpec as P

LEAVES = 256
STEP = 2048
HESS, GRAD, HESS_ALL, GRAD_ALL, HESS_UNIT, GRAD_UNIT = 1, 2, 3, 4, 5, 6
F32, BF16, F16, I32 = jnp.float32, jnp.bfloat16, jnp.float16, jnp.int32
NT = (((1,), (1,)), ((), ()))


def pair_layout(regress):
    subs, first = [], {}
    for a in range(0, regress, 2):
        blocks = a // 8 + 1
        for one in (a, a + 1):
            for m in range(blocks // 2):
                first[one, 2 * m] = 16 * len(subs)
                first[one, 2 * m + 1] = 16 * len(subs) + 8
                subs.append(("full", one, m))
        if blocks % 2:
            first[a, blocks - 1] = 16 * len(subs)
            first[a + 1, blocks - 1] = 16 * len(subs) + 8
            subs.append(("half", a, blocks - 1))
    return subs, first


def sums_kernel(subs, out_width, step, me_ref, range_ref, feat_hbm, hess_hbm, grad_hbm, leaf_hbm, keep_ref, send_ref, feat_all, hess_all, grad_all, leaf_all, w_ref, total_ref, sems):
    regress, rows = feat_all.shape
    copies = [
        pltpu.make_async_copy(source, target, sems.at[i])
        for i, (source, target) in enumerate(((feat_hbm, feat_all), (hess_hbm, hess_all), (grad_hbm, grad_all), (leaf_hbm, leaf_all)))
    ]
    for copy in copies:
        copy.start()
    total_ref[...] = jnp.zeros_like(total_ref)
    for copy in copies:
        copy.wait()

    def chunk(k, fresh):
        at = pl.ds(k * step if isinstance(k, int) else pl.multiple_of(k * step, step), step)
        position = me_ref[1] + k * step + lax.broadcasted_iota(I32, (1, step), 1)
        inside = jnp.where((position >= range_ref[0]) & (position < range_ref[1]), 1.0, 0.0)
        hess = hess_all[:, at] * inside
        grad = (grad_all[:, at] * inside).astype(BF16)
        hess_b = hess.astype(BF16)
        leaf = leaf_all[:, at] ^ me_ref[0]
        hot = jnp.where(lax.broadcasted_iota(I32, (LEAVES, step), 0) == leaf, 1.0, 0.0).astype(BF16)
        feat = feat_all[:, at]
        feat_f = feat.astype(F32)
        w_ref[...] = feat_f * hess

        @functools.lru_cache(None)
        def weight(a, count):
            return jnp.broadcast_to(w_ref[a:a + 1, :], (count, step))

        @functools.lru_cache(None)
        def weight_b(a):
            return weight(a, 16).astype(BF16)

        @functools.lru_cache(None)
        def twice(m):
            part = feat_f[8 * m:8 * m + 8]
            return jnp.concatenate([part, part], 0).astype(BF16)

        def rows_of(sub):
            kind, a, m = sub
            if kind == "full":
                return weight_b(a) * feat[16 * m:16 * m + 16]
            if kind == "half":
                both = jnp.concatenate([weight(a, 8), weight(a + 1, 8)], 0).astype(BF16)
                tile = both * twice(m)
                if a == 0:
                    row = lax.broadcasted_iota(I32, (16, step), 0)
                    tile_f = tile.astype(F32)
                    tile_f = jnp.where(row == HESS, hess_b.astype(F32), tile_f)
                    tile_f = jnp.where(row == GRAD, grad.astype(F32), tile_f)
                    tile = tile_f.astype(BF16)
                return tile
            if kind == "weight":
                return w_ref[16 * m:16 * m + 16, :].astype(BF16)
            if kind == "zero":
                return jnp.zeros((16, step), BF16)
            exact = feat_f[16 * m:16 * m + 16] * grad.astype(F32)
            high = exact.astype(BF16)
            if kind == "grad_high":
                return high
            return (exact - high.astype(F32)).astype(BF16)

        for t in range(len(subs) * 16 // 256):
            tile = jnp.concatenate([rows_of(s) for s in subs[16 * t:16 * t + 16]], 0)
            part = lax.dot_general(hot, tile, NT, preferred_element_type=F32)
            if (t + 1) * 256 > out_width:
                part = part[:, :128] + part[:, 128:]
            lanes = slice(t * 256, t * 256 + part.shape[1])
            if fresh:
                keep_ref[:, lanes] = part[:LEAVES // 2]
                send_ref[:, lanes] = part[LEAVES // 2:]
            else:
                keep_ref[:, lanes] += part[:LEAVES // 2]
                send_ref[:, lanes] += part[LEAVES // 2:]
        total_ref[0:1, :] += hess_b.astype(F32)
        total_ref[1:2, :] += jnp.abs(grad.astype(F32))

    chunk(0, True)
    if rows > step:
        lax.fori_loop(1, rows // step, lambda k, carry: (chunk(k, False), carry)[1], 0)
    hess_total, grad_total = jnp.sum(total_ref[0:1, :]), jnp.sum(total_ref[1:2, :])
    lane = lax.broadcasted_iota(I32, (LEAVES // 2, 128), 1)
    for ref in (keep_ref, send_ref):
        first = jnp.where(lane == HESS_ALL, hess_total, ref[:, :128])
        ref[:, :128] = jnp.where(lane == GRAD_ALL, grad_total, first)


def sums_call(subs, out_width, step, me, train_range, features, hessian, gradient, leaf):
    regress, rows = features.shape
    return pl.pallas_call(
        functools.partial(sums_kernel, subs, out_width, step),
        in_specs=[pl.BlockSpec(memory_space=pltpu.SMEM)] * 2 + [pl.BlockSpec(memory_space=pl.ANY)] * 4,
        out_specs=[pl.BlockSpec(memory_space=pltpu.VMEM)] * 2,
        out_shape=[jax.ShapeDtypeStruct((LEAVES // 2, out_width), F32)] * 2,
        scratch_shapes=[
            pltpu.VMEM((regress, rows), BF16),
            pltpu.VMEM((1, rows), F32),
            pltpu.VMEM((1, rows), F32),
            pltpu.VMEM((1, rows), I32),
            pltpu.VMEM((regress, step), F32),
            pltpu.VMEM((2, step), F32),
            pltpu.SemaphoreType.DMA((4,)),
        ],
        compiler_params=pltpu.CompilerParams(vmem_limit_bytes=56 << 20),
        cost_estimate=pl.CostEstimate(flops=2 * LEAVES * rows * len(subs) * 16, bytes_accessed=rows * 144 + LEAVES * out_width * 4, transcendentals=0),
    )(me, train_range, features, hessian, gradient, leaf)


def solve_kernel(regress, first, sums_ref, out_ref, t_ref, u_ref, z_ref, c_ref):
    held = sums_ref.shape[0]
    for lane in range(0, sums_ref.shape[1], 128):
        tile = jnp.concatenate([sums_ref[:, lane:lane + 128], jnp.zeros((128 - held, 128), F32)], 0)
        t_ref[lane:lane + 128, :] = tile.T
    last = regress
    first = dict(first)
    for m in range(regress // 8):
        first[last, m] = starts_of_last(regress) + 8 * m
    grad_at = starts_of_last(regress) + regress
    corner = t_ref[first[0, 0]:first[0, 0] + 8, :]
    real = lax.broadcasted_iota(I32, (1, 128), 1) < held
    ridge = jnp.where(real, corner[3:4] * (0.5 / LEAVES), 1.0)
    blocks = regress // 8

    def row(a, m):
        return t_ref[first[a, m]:first[a, m] + 8, :]

    def pivot(a, own, count):
        inverse = 1.0 / (own + ridge)
        for m in range(count):
            u_ref[a, 8 * m:8 * m + 8, :] = row(a, m) * inverse
        return inverse

    def reduce_target(a, inverse, value):
        scaled = value * inverse
        z_ref[a:a + 1, :] = scaled
        for m in range((a + 7) // 8):
            t_ref[grad_at + 8 * m:grad_at + 8 * m + 8, :] -= row(a, m) * scaled

    for m in range(blocks):
        t_ref[grad_at + 8 * m:grad_at + 8 * m + 8, :] = -t_ref[grad_at + 8 * m:grad_at + 8 * m + 8, :]
    inverse = pivot(last, corner[1:2], blocks)
    reduce_target(last, inverse, -corner[2:3])
    for q in range(blocks - 1, -1, -1):
        for top in (8 * q + 4, 8 * q):
            some = range(top + 3, top - 1, -1)
            total = {(a, m): row(a, m) for a in some for m in range(q + 1)}
            for k in range(last, 8 * q + 7, -1):
                line = [row(k, m) for m in range(q + 1)]
                for a in some:
                    scale = u_ref[k, a:a + 1, :]
                    for m in range(q + 1):
                        total[a, m] = total[a, m] - scale * line[m]
            for (a, m), value in total.items():
                t_ref[first[a, m]:first[a, m] + 8, :] = value
        for a in range(8 * q + 7, 8 * q - 1, -1):
            total = [row(a, m) for m in range(q + 1)]
            for k in range(8 * q + 7, a, -1):
                scale = u_ref[k, a:a + 1, :]
                for m in range(q + 1):
                    total[m] = total[m] - scale * row(k, m)
            for m in range(q + 1):
                t_ref[first[a, m]:first[a, m] + 8, :] = total[m]
            at = first[a, q] + a % 8
            inverse = pivot(a, t_ref[at:at + 1, :], q + 1)
            reduce_target(a, inverse, t_ref[grad_at + a:grad_at + a + 1, :])
    c_ref[...] = jnp.zeros_like(c_ref)
    for q in range(blocks + 1):
        rows = range(8 * q, min(8 * q + 8, regress + 1))
        known = {}
        for k in rows:
            value = z_ref[k:k + 1, :]
            if q:
                products = u_ref[k, 0:8, :] * c_ref[0:8, :]
                for m in range(1, q):
                    products = products + u_ref[k, 8 * m:8 * m + 8, :] * c_ref[8 * m:8 * m + 8, :]
                value = value - jnp.sum(products, 0, keepdims=True)
            known[k] = value
        for k in rows:
            for b in range(8 * q, k):
                known[k] = known[k] - u_ref[k, b:b + 1, :] * known[b]
        for k in rows:
            c_ref[k:k + 1, :] = known[k]
    out_ref[...] = c_ref[...].T[:held]


def starts_of_last(regress):
    return 16 * len(pair_layout(regress)[0])


def solve_call(regress, sums):
    held, lanes = sums.shape
    return pl.pallas_call(
        functools.partial(solve_kernel, regress, pair_layout(regress)[1]),
        out_shape=jax.ShapeDtypeStruct((held, 128), F32),
        in_specs=[pl.BlockSpec(memory_space=pltpu.VMEM)],
        out_specs=pl.BlockSpec(memory_space=pltpu.VMEM),
        scratch_shapes=[
            pltpu.VMEM((lanes, 128), F32),
            pltpu.VMEM((regress + 1, regress, 128), F32),
            pltpu.VMEM((72, 128), F32),
            pltpu.VMEM((128, 128), F32),
        ],
        compiler_params=pltpu.CompilerParams(vmem_limit_bytes=32 << 20),
    )(sums)


def apply_kernel(places, block, step, me_ref, *refs):
    part_refs = refs[:len(places)]
    feat_ref, hess_ref, grad_ref, leaf_ref, coef_ref, next_ref, real_ref = refs[len(places):]
    regress, rows = feat_ref.shape
    for ref, owners in zip(part_refs, places):
        for at, place in enumerate(owners):
            target = pl.multiple_of((place * block) ^ me_ref[0], block)
            real_ref[pl.ds(target, block), :] = ref[at * block:(at + 1) * block, :]
    turned = real_ref[...].T
    coef_ref[...] = turned[:regress + 1]
    high = turned[:80].astype(BF16)
    low = (turned[:80] - high.astype(F32)).astype(BF16)
    for start in range(0, rows, step):
        at = slice(start, start + step)
        hot = jnp.where(lax.broadcasted_iota(I32, (LEAVES, step), 0) == leaf_ref[:, at], 1.0, 0.0).astype(BF16)
        picked = jnp.dot(high, hot, preferred_element_type=F32) + jnp.dot(low, hot, preferred_element_type=F32)
        predicted = jnp.sum(picked[:regress] * feat_ref[:, at].astype(F32), 0, keepdims=True) + picked[regress:regress + 1]
        next_ref[:, at] = grad_ref[:, at] + hess_ref[:, at] * predicted


def apply_call(places, block, parts, step, me, features, hessian, gradient, leaf):
    regress, rows = features.shape
    return pl.pallas_call(
        functools.partial(apply_kernel, places, block, step),
        in_specs=[pl.BlockSpec(memory_space=pltpu.SMEM)] + [pl.BlockSpec(memory_space=pltpu.VMEM)] * (len(parts) + 4),
        out_specs=[pl.BlockSpec(memory_space=pltpu.VMEM)] * 2,
        out_shape=[jax.ShapeDtypeStruct((regress + 1, LEAVES), F32), jax.ShapeDtypeStruct((1, rows), F32)],
        scratch_shapes=[pltpu.VMEM((LEAVES, 128), F32)],
        compiler_params=pltpu.CompilerParams(vmem_limit_bytes=32 << 20),
    )(me, *parts, features, hessian, gradient, leaf)


def grad_lanes(regress, lanes):
    lane = lax.broadcasted_iota(I32, (1, lanes), 1)
    return (lane == GRAD) | (lane == GRAD_ALL) | (lane >= starts_of_last(regress) + regress)


def encode(regress, x):
    lane = lax.broadcasted_iota(I32, (1, x.shape[1]), 1)
    hess_unit = jnp.clip(jnp.ceil(jnp.log2(x[:, HESS_ALL:HESS_ALL + 1] * (36.0 / 50000.0))), -100.0, 100.0)
    grad_unit = jnp.clip(jnp.ceil(jnp.log2(x[:, GRAD_ALL:GRAD_ALL + 1] * (6.0 / 50000.0))), -100.0, 100.0)
    y = x * jnp.where(grad_lanes(regress, x.shape[1]), jnp.exp2(-grad_unit), jnp.exp2(-hess_unit))
    y = jnp.where(lane == HESS_UNIT, hess_unit, jnp.where(lane == GRAD_UNIT, grad_unit, y))
    return lax.optimization_barrier(y.astype(F16))


def decode(regress, y):
    y = y.astype(F32)
    hess_unit, grad_unit = y[:, HESS_UNIT:HESS_UNIT + 1], y[:, GRAD_UNIT:GRAD_UNIT + 1]
    return y * jnp.where(grad_lanes(regress, y.shape[1]), jnp.exp2(grad_unit), jnp.exp2(hess_unit))


def row_groups(bits):
    return [(shift, min(2, bits - shift)) for shift in range(0, bits, 2)]


def swap_rows(x, rows, distance):
    return lax.ppermute(x, "row", [(r, r ^ distance) for r in range(rows)])


def body(features, hessian, gradient, leaf_index, train_range):
    regress, local = features.shape
    rows = lax.axis_size("row")
    bits = rows.bit_length() - 1
    groups = row_groups(bits - 1)
    block = LEAVES >> bits
    row, core = lax.axis_index("row"), lax.axis_index("leaf")

    def place_of(core, row):
        place = core
        for shift, count in groups:
            place = (place << count) | ((row >> shift) & ((1 << count) - 1))
        return place

    me = jnp.stack([place_of(core, row) * block, (row * 2 + core) * local]).astype(I32)
    rowed = [hessian.reshape(1, local), gradient.reshape(1, local), leaf_index.reshape(1, local)]
    subs, first = pair_layout(regress)
    count = regress // 16
    subs = subs + [("weight", 0, m) for m in range(count)] + [("grad_high", 0, m) for m in range(count)]
    subs = subs + [("zero", 0, 0)] * count + [("grad_low", 0, m) for m in range(count)]
    keep, send = sums_call(subs, len(subs) * 16 - 128, STEP, me, train_range, features, *rowed)
    sums = keep + lax.ppermute(send, "leaf", [(0, 1), (1, 0)])
    for shift, count in groups:
        size = sums.shape[0] >> count
        got = [swap_rows(encode(regress, sums[d * size:(d + 1) * size]), rows, d << shift) for d in range(1, 1 << count)]
        sums = sum([decode(regress, x) for x in got], sums[:size])
    mine = encode(regress, sums)
    sums = decode(regress, mine) + decode(regress, swap_rows(mine, rows, rows // 2))
    if block % 8:
        sums = jnp.pad(sums, ((0, -block % 8), (0, 0)))
    coef = solve_call(regress, sums)[:block]
    both = jnp.concatenate([coef, lax.ppermute(coef, "leaf", [(0, 1), (1, 0)])], 0)
    held = [([0], both)]
    for shift, count in groups:
        names = [d for owners, _ in held for d in owners]
        array = jnp.concatenate([x for _, x in held], 0) if len(held) > 1 else held[0][1]
        held = held + [([n ^ (d << shift) for n in names], swap_rows(array, rows, d << shift)) for d in range(1, 1 << count)]
    places = [[place_of(c, d) for d in owners for c in range(2)] for owners, _ in held]
    coefficients, following = apply_call(places, block, [x for _, x in held], STEP, me, features, *rowed)
    return coefficients.T, following.reshape(local)


def solution(mesh):
    placed = (
        P(None, ("fold", "row", "leaf")),
        P(("fold", "row", "leaf")),
        P(("fold", "row", "leaf")),
        P(("fold", "row", "leaf"), None),
        P("fold"),
    )
    return jax.shard_map(
        body,
        mesh=mesh,
        in_specs=placed,
        out_specs=(P("fold", None), P(("fold", "row", "leaf"))),
        check_vma=False,
    )
```

```python
import functools
import jax
import jax.numpy as jnp
from jax import lax
from jax.experimental import pallas as pl
from jax.experimental.pallas import tpu as pltpu
from jax.sharding import PartitionSpec as P

LEAVES = 256
STEP = 2048
CALLS = (((0, 7), (7, 10)),)
HESS, GRAD, HESS_ALL, GRAD_ALL, HESS_UNIT, GRAD_UNIT = 1, 2, 3, 4, 5, 6
F32, BF16, F16, I32 = jnp.float32, jnp.bfloat16, jnp.float16, jnp.int32
NT = (((1,), (1,)), ((), ()))


def pair_layout(regress):
    subs, first = [], {}
    for a in range(0, regress, 2):
        blocks = a // 8 + 1
        for one in (a, a + 1):
            for m in range(blocks // 2):
                first[one, 2 * m] = 16 * len(subs)
                first[one, 2 * m + 1] = 16 * len(subs) + 8
                subs.append(("full", one, m))
        if blocks % 2:
            first[a, blocks - 1] = 16 * len(subs)
            first[a + 1, blocks - 1] = 16 * len(subs) + 8
            subs.append(("half", a, blocks - 1))
    return subs, first


def row_groups(bits):
    return [(shift, min(2, bits - shift)) for shift in range(0, bits, 2)]


def place_of(bits, core, row):
    place = core
    for shift, count in row_groups(bits - 1):
        place = (place << count) | ((row >> shift) & ((1 << count) - 1))
    return place


def own_leaves(bits):
    return place_of(bits, lax.axis_index("leaf"), lax.axis_index("row")) * (LEAVES >> bits)


def add_tiles(subs, out_width, step, range_ref, feat_all, hess_all, grad_all, hot_all, keep_ref, send_ref, w_ref, before, after):
    regress, rows = feat_all.shape
    origin = (lax.axis_index("row") * 2 + lax.axis_index("leaf")) * rows

    def chunk(k, fresh):
        at = pl.ds(k * step if isinstance(k, int) else pl.multiple_of(k * step, step), step)
        before(k, at)
        position = origin + k * step + lax.broadcasted_iota(I32, (1, step), 1)
        inside = jnp.where((position >= range_ref[0]) & (position < range_ref[1]), 1.0, 0.0)
        hess = hess_all[:, at] * inside
        grad = (grad_all[:, at] * inside).astype(BF16)
        hess_b = hess.astype(BF16)
        hot = hot_all[:, at]
        feat = feat_all[:, at]
        feat_f = feat.astype(F32)
        w_ref[...] = feat_f * hess

        @functools.lru_cache(None)
        def weight(a, count):
            return jnp.broadcast_to(w_ref[a:a + 1, :], (count, step))

        @functools.lru_cache(None)
        def weight_b(a):
            return weight(a, 16).astype(BF16)

        @functools.lru_cache(None)
        def twice(m):
            part = feat_f[8 * m:8 * m + 8]
            return jnp.concatenate([part, part], 0).astype(BF16)

        def rows_of(sub):
            kind, a, m = sub
            if kind == "full":
                return weight_b(a) * feat[16 * m:16 * m + 16]
            if kind == "half":
                both = jnp.concatenate([weight(a, 8), weight(a + 1, 8)], 0).astype(BF16)
                tile = both * twice(m)
                if a == 0:
                    row = lax.broadcasted_iota(I32, (16, step), 0)
                    tile_f = tile.astype(F32)
                    tile_f = jnp.where(row == HESS, hess_b.astype(F32), tile_f)
                    tile_f = jnp.where(row == GRAD, grad.astype(F32), tile_f)
                    tile = tile_f.astype(BF16)
                return tile
            if kind == "weight":
                return w_ref[16 * m:16 * m + 16, :].astype(BF16)
            if kind == "zero":
                return jnp.zeros((16, step), BF16)
            exact = feat_f[16 * m:16 * m + 16] * grad.astype(F32)
            high = exact.astype(BF16)
            if kind == "grad_high":
                return high
            return (exact - high.astype(F32)).astype(BF16)

        for t in range(len(subs) * 16 // 256):
            tile = jnp.concatenate([rows_of(s) for s in subs[16 * t:16 * t + 16]], 0)
            part = lax.dot_general(hot, tile, NT, preferred_element_type=F32)
            if (t + 1) * 256 > out_width:
                part = part[:, :128] + part[:, 128:]
            lanes = slice(t * 256, t * 256 + part.shape[1])
            if fresh:
                keep_ref[:, lanes] = part[:LEAVES // 2]
                send_ref[:, lanes] = part[LEAVES // 2:]
            else:
                keep_ref[:, lanes] += part[:LEAVES // 2]
                send_ref[:, lanes] += part[LEAVES // 2:]
        after(hess_b.astype(F32), jnp.abs(grad.astype(F32)))

    chunk(0, True)
    if rows > step:
        lax.fori_loop(1, rows // step, lambda k, carry: (chunk(k, False), carry)[1], 0)


def first_kernel(subs, out_width, step, bits, range_ref, feat_hbm, hess_hbm, grad_hbm, leaf_hbm, keep_ref, send_ref, hot_all, feat_all, hess_all, grad_all, leaf_all, w_ref, total_ref, sems, feat_sems):
    rows = feat_all.shape[1]
    copies = [
        pltpu.make_async_copy(source, target, sems.at[i])
        for i, (source, target) in enumerate(((leaf_hbm, leaf_all), (hess_hbm, hess_all), (grad_hbm, grad_all)))
    ]

    def feat_copy(k):
        at = pl.ds(k * step if isinstance(k, int) else pl.multiple_of(k * step, step), step)
        return pltpu.make_async_copy(feat_hbm.at[:, at], feat_all.at[:, at], feat_sems.at[k])

    for copy in copies:
        copy.start()
    for k in range(rows // step):
        feat_copy(k).start()
    total_ref[...] = jnp.zeros_like(total_ref)
    for copy in copies:
        copy.wait()
    own = own_leaves(bits)

    def before(k, at):
        leaf = leaf_all[:, at] ^ own
        hot_all[:, at] = jnp.where(lax.broadcasted_iota(I32, (LEAVES, step), 0) == leaf, 1.0, 0.0).astype(BF16)
        feat_copy(k).wait()

    def after(hess, grad):
        total_ref[0:1, :] += hess
        total_ref[1:2, :] += grad

    add_tiles(subs, out_width, step, range_ref, feat_all, hess_all, grad_all, hot_all, keep_ref, send_ref, w_ref, before, after)
    hess_total, grad_total = jnp.sum(total_ref[0:1, :]), jnp.sum(total_ref[1:2, :])
    lane = lax.broadcasted_iota(I32, (LEAVES // 2, 128), 1)
    for ref in (keep_ref, send_ref):
        first = jnp.where(lane == HESS_ALL, hess_total, ref[:, :128])
        ref[:, :128] = jnp.where(lane == GRAD_ALL, grad_total, first)


def later_kernel(subs, out_width, step, range_ref, hot_all, feat_all, hess_all, grad_all, keep_ref, send_ref, w_ref):
    nothing = lambda *ignored: None
    add_tiles(subs, out_width, step, range_ref, feat_all, hess_all, grad_all, hot_all, keep_ref, send_ref, w_ref, nothing, nothing)


def sums_cost(subs, out_width, rows):
    return pl.CostEstimate(flops=2 * LEAVES * rows * len(subs) * 16, bytes_accessed=rows * 656 + LEAVES * out_width * 4, transcendentals=0)


def first_call(subs, out_width, step, bits, train_range, features, hessian, gradient, leaf):
    regress, rows = features.shape
    return pl.pallas_call(
        functools.partial(first_kernel, subs, out_width, step, bits),
        in_specs=[pl.BlockSpec(memory_space=pltpu.SMEM)] + [pl.BlockSpec(memory_space=pltpu.HBM)] * 4,
        out_specs=[pl.BlockSpec(memory_space=pltpu.VMEM)] * 6,
        out_shape=[jax.ShapeDtypeStruct((LEAVES // 2, out_width), F32)] * 2
        + [jax.ShapeDtypeStruct((LEAVES, rows), BF16), jax.ShapeDtypeStruct((regress, rows), BF16)]
        + [jax.ShapeDtypeStruct((1, rows), F32)] * 2,
        scratch_shapes=[
            pltpu.VMEM((1, rows), I32),
            pltpu.VMEM((regress, step), F32),
            pltpu.VMEM((2, step), F32),
            pltpu.SemaphoreType.DMA((3,)),
            pltpu.SemaphoreType.DMA((rows // step,)),
        ],
        compiler_params=pltpu.CompilerParams(vmem_limit_bytes=28 << 20),
        cost_estimate=sums_cost(subs, out_width, rows),
    )(*[pltpu.with_memory_space_constraint(x, pltpu.HBM) for x in (train_range, features, hessian, gradient, leaf)])


def later_call(subs, out_width, step, train_range, hot, features, hessian, gradient):
    regress, rows = features.shape
    return pl.pallas_call(
        functools.partial(later_kernel, subs, out_width, step),
        in_specs=[pl.BlockSpec(memory_space=pltpu.SMEM)] + [pl.BlockSpec(memory_space=pltpu.VMEM)] * 4,
        out_specs=[pl.BlockSpec(memory_space=pltpu.VMEM)] * 2,
        out_shape=[jax.ShapeDtypeStruct((LEAVES // 2, out_width), F32)] * 2,
        scratch_shapes=[pltpu.VMEM((regress, step), F32)],
        compiler_params=pltpu.CompilerParams(vmem_limit_bytes=28 << 20),
        cost_estimate=sums_cost(subs, out_width, rows),
    )(train_range, hot, features, hessian, gradient)


def solve_kernel(regress, first, sums_ref, out_ref, t_ref, u_ref, z_ref, c_ref):
    held = sums_ref.shape[0]
    for lane in range(0, sums_ref.shape[1], 128):
        tile = jnp.concatenate([sums_ref[:, lane:lane + 128], jnp.zeros((128 - held, 128), F32)], 0)
        t_ref[lane:lane + 128, :] = tile.T
    last = regress
    first = dict(first)
    for m in range(regress // 8):
        first[last, m] = starts_of_last(regress) + 8 * m
    grad_at = starts_of_last(regress) + regress
    corner = t_ref[first[0, 0]:first[0, 0] + 8, :]
    real = lax.broadcasted_iota(I32, (1, 128), 1) < held
    ridge = jnp.where(real, corner[3:4] * (0.5 / LEAVES), 1.0)
    blocks = regress // 8

    def row(a, m):
        return t_ref[first[a, m]:first[a, m] + 8, :]

    def pivot(a, own, count):
        inverse = 1.0 / (own + ridge)
        for m in range(count):
            u_ref[a, 8 * m:8 * m + 8, :] = row(a, m) * inverse
        return inverse

    def reduce_target(a, inverse, value):
        scaled = value * inverse
        z_ref[a:a + 1, :] = scaled
        for m in range((a + 7) // 8):
            t_ref[grad_at + 8 * m:grad_at + 8 * m + 8, :] -= row(a, m) * scaled

    for m in range(blocks):
        t_ref[grad_at + 8 * m:grad_at + 8 * m + 8, :] = -t_ref[grad_at + 8 * m:grad_at + 8 * m + 8, :]
    inverse = pivot(last, corner[1:2], blocks)
    reduce_target(last, inverse, -corner[2:3])
    for q in range(blocks - 1, -1, -1):
        for top in (8 * q + 4, 8 * q):
            some = range(top + 3, top - 1, -1)
            total = {(a, m): row(a, m) for a in some for m in range(q + 1)}
            for k in range(last, 8 * q + 7, -1):
                line = [row(k, m) for m in range(q + 1)]
                for a in some:
                    scale = u_ref[k, a:a + 1, :]
                    for m in range(q + 1):
                        total[a, m] = total[a, m] - scale * line[m]
            for (a, m), value in total.items():
                t_ref[first[a, m]:first[a, m] + 8, :] = value
        for a in range(8 * q + 7, 8 * q - 1, -1):
            total = [row(a, m) for m in range(q + 1)]
            for k in range(8 * q + 7, a, -1):
                scale = u_ref[k, a:a + 1, :]
                for m in range(q + 1):
                    total[m] = total[m] - scale * row(k, m)
            for m in range(q + 1):
                t_ref[first[a, m]:first[a, m] + 8, :] = total[m]
            at = first[a, q] + a % 8
            inverse = pivot(a, t_ref[at:at + 1, :], q + 1)
            reduce_target(a, inverse, t_ref[grad_at + a:grad_at + a + 1, :])
    c_ref[...] = jnp.zeros_like(c_ref)
    for q in range(blocks + 1):
        rows = range(8 * q, min(8 * q + 8, regress + 1))
        known = {}
        for k in rows:
            value = z_ref[k:k + 1, :]
            if q:
                products = u_ref[k, 0:8, :] * c_ref[0:8, :]
                for m in range(1, q):
                    products = products + u_ref[k, 8 * m:8 * m + 8, :] * c_ref[8 * m:8 * m + 8, :]
                value = value - jnp.sum(products, 0, keepdims=True)
            known[k] = value
        for k in rows:
            for b in range(8 * q, k):
                known[k] = known[k] - u_ref[k, b:b + 1, :] * known[b]
        for k in rows:
            c_ref[k:k + 1, :] = known[k]
    out_ref[...] = c_ref[...].T[:held]


def starts_of_last(regress):
    return 16 * len(pair_layout(regress)[0])


def solve_call(regress, sums):
    held, lanes = sums.shape
    return pl.pallas_call(
        functools.partial(solve_kernel, regress, pair_layout(regress)[1]),
        out_shape=jax.ShapeDtypeStruct((held, 128), F32),
        in_specs=[pl.BlockSpec(memory_space=pltpu.VMEM)],
        out_specs=pl.BlockSpec(memory_space=pltpu.VMEM),
        scratch_shapes=[
            pltpu.VMEM((lanes, 128), F32),
            pltpu.VMEM((regress + 1, regress, 128), F32),
            pltpu.VMEM((72, 128), F32),
            pltpu.VMEM((128, 128), F32),
        ],
        compiler_params=pltpu.CompilerParams(vmem_limit_bytes=32 << 20),
    )(sums)


def apply_kernel(places, block, step, bits, *refs):
    part_refs = refs[:len(places)]
    hot_ref, feat_ref, hess_ref, grad_ref, coef_ref, next_ref, real_ref, own_ref = refs[len(places):]
    regress, rows = feat_ref.shape
    own = own_leaves(bits)
    for ref, owners in zip(part_refs, places):
        for at, place in enumerate(owners):
            value = ref[at * block:(at + 1) * block, :]
            own_ref[place * block:(place + 1) * block, :] = value
            real_ref[pl.ds(pl.multiple_of((place * block) ^ own, block), block), :] = value
    turned = own_ref[...].T[:80]
    high = turned.astype(BF16)
    both = jnp.concatenate([high, (turned - high.astype(F32)).astype(BF16)], 0)
    for start in range(0, rows, step):
        at = slice(start, start + step)
        picked = jnp.dot(both, hot_ref[:, at], preferred_element_type=F32)
        picked = picked[:80] + picked[80:]
        predicted = jnp.sum(picked[:regress] * feat_ref[:, at].astype(F32), 0, keepdims=True) + picked[regress:regress + 1]
        next_ref[:, at] = grad_ref[:, at] + hess_ref[:, at] * predicted
    coef_ref[...] = real_ref[...].T[:regress + 1]


def apply_call(places, block, parts, step, bits, hot, features, hessian, gradient):
    regress, rows = features.shape
    return pl.pallas_call(
        functools.partial(apply_kernel, places, block, step, bits),
        in_specs=[pl.BlockSpec(memory_space=pltpu.VMEM)] * (len(parts) + 4),
        out_specs=[pl.BlockSpec(memory_space=pltpu.VMEM)] * 2,
        out_shape=[jax.ShapeDtypeStruct((regress + 1, LEAVES), F32), jax.ShapeDtypeStruct((1, rows), F32)],
        scratch_shapes=[pltpu.VMEM((LEAVES, 128), F32), pltpu.VMEM((LEAVES, 128), F32)],
        compiler_params=pltpu.CompilerParams(vmem_limit_bytes=28 << 20),
    )(*parts, hot, features, hessian, gradient)


def grad_lanes(regress, start, lanes):
    lane = start + lax.broadcasted_iota(I32, (1, lanes), 1)
    return (lane == GRAD) | (lane == GRAD_ALL) | (lane >= starts_of_last(regress) + regress)


def units_of(x):
    hess = jnp.clip(jnp.ceil(jnp.log2(x[:, HESS_ALL:HESS_ALL + 1] * (36.0 / 50000.0))), -100.0, 100.0)
    grad = jnp.clip(jnp.ceil(jnp.log2(x[:, GRAD_ALL:GRAD_ALL + 1] * (6.0 / 50000.0))), -100.0, 100.0)
    return hess, grad


def encode(regress, start, x, units):
    y = x * jnp.where(grad_lanes(regress, start, x.shape[1]), jnp.exp2(-units[1]), jnp.exp2(-units[0]))
    if start == 0:
        lane = lax.broadcasted_iota(I32, (1, x.shape[1]), 1)
        y = jnp.where(lane == HESS_UNIT, units[0], jnp.where(lane == GRAD_UNIT, units[1], y))
    return lax.optimization_barrier(y.astype(F16))


def decode(regress, start, y, units):
    return y.astype(F32) * jnp.where(grad_lanes(regress, start, y.shape[1]), jnp.exp2(units[1]), jnp.exp2(units[0]))


def carried(y):
    return y[:, HESS_UNIT:HESS_UNIT + 1].astype(F32), y[:, GRAD_UNIT:GRAD_UNIT + 1].astype(F32)


def swap_rows(x, rows, distance):
    return lax.ppermute(x, "row", [(r, r ^ distance) for r in range(rows)])


def body(features, hessian, gradient, leaf_index, train_range):
    regress, local = features.shape
    rows = lax.axis_size("row")
    bits = rows.bit_length() - 1
    groups = row_groups(bits - 1)
    block = LEAVES >> bits
    subs, first = pair_layout(regress)
    count = regress // 16
    subs = subs + [("weight", 0, m) for m in range(count)] + [("grad_high", 0, m) for m in range(count)]
    subs = subs + [("zero", 0, 0)] * count + [("grad_low", 0, m) for m in range(count)]
    kept, shared, previous = [], None, None
    units = [None] * (len(groups) + 1)
    for calls in CALLS:
        pieces = []
        for begin, end in calls:
            part = subs[16 * begin:16 * end]
            width = 256 * (end - begin) - (128 if 16 * end == len(subs) else 0)
            if shared is None:
                keep, send, *shared = first_call(part, width, STEP, bits, train_range, features, hessian.reshape(1, local), gradient.reshape(1, local), leaf_index.reshape(1, local))
            else:
                train_range, previous = lax.optimization_barrier((train_range, previous))
                keep, send = later_call(part, width, STEP, train_range, *shared)
            previous = send
            pieces.append(keep + lax.ppermute(send, "leaf", [(0, 1), (1, 0)]))
        start = 256 * calls[0][0]
        sums = jnp.concatenate(pieces, 1) if len(pieces) > 1 else pieces[0]
        for level, (shift, count) in enumerate(groups):
            size = sums.shape[0] >> count
            own = units_of(sums[:size]) if start == 0 else units[level][0]
            sent = [encode(regress, start, sums[d * size:(d + 1) * size], own) for d in range(1, 1 << count)]
            previous = sent[0]
            got = [swap_rows(x, rows, d << shift) for x, d in zip(sent, range(1, 1 << count))]
            if start == 0:
                units[level] = [own] + [carried(x) for x in got]
            sums = sum([decode(regress, start, x, u) for x, u in zip(got, units[level][1:])], sums[:size])
        own = units_of(sums) if start == 0 else units[-1][0]
        mine = encode(regress, start, sums, own)
        other = swap_rows(mine, rows, rows // 2)
        if start == 0:
            units[-1] = [own, carried(other)]
        kept.append(decode(regress, start, mine, units[-1][0]) + decode(regress, start, other, units[-1][1]))
    sums = jnp.concatenate(kept, 1) if len(kept) > 1 else kept[0]
    if block % 8:
        sums = jnp.pad(sums, ((0, -block % 8), (0, 0)))
    coef = solve_call(regress, sums)[:block]
    both = jnp.concatenate([coef, lax.ppermute(coef, "leaf", [(0, 1), (1, 0)])], 0)
    held = [([0], both)]
    for shift, count in groups:
        names = [d for owners, _ in held for d in owners]
        array = jnp.concatenate([x for _, x in held], 0) if len(held) > 1 else held[0][1]
        held = held + [([n ^ (d << shift) for n in names], swap_rows(array, rows, d << shift)) for d in range(1, 1 << count)]
    places = [[place_of(bits, c, d) for d in owners for c in range(2)] for owners, _ in held]
    coefficients, following = apply_call(places, block, [x for _, x in held], STEP, bits, *shared)
    return coefficients.T, following.reshape(local)


def solution(mesh):
    placed = (
        P(None, ("fold", "row", "leaf")),
        P(("fold", "row", "leaf")),
        P(("fold", "row", "leaf")),
        P(("fold", "row", "leaf"), None),
        P("fold"),
    )
    return jax.shard_map(
        body,
        mesh=mesh,
        in_specs=placed,
        out_specs=(P("fold", None), P(("fold", "row", "leaf"))),
        check_vma=False,
    )
```

```python
import functools
import jax
import jax.numpy as jnp
from jax import lax
from jax.experimental import pallas as pl
from jax.experimental.pallas import tpu as pltpu
from jax.sharding import PartitionSpec as P

LEAVES = 256
FIRST_STEP, LATER_STEP, APPLY_STEP = 2048, 4096, 2048
CALLS = ((0, 6), (6, 9))
HESS, GRAD, HESS_ALL, GRAD_ALL, HESS_UNIT, GRAD_UNIT = 28, 29, 30, 31, 60, 61
F32, BF16, F16, I32 = jnp.float32, jnp.bfloat16, jnp.float16, jnp.int32
NT = (((1,), (1,)), ((), ()))


def pair_layout(regress):
    subs, first, inner = [], {}, {}
    for q in range(regress // 8):
        for j in (0, 2):
            at = 16 * len(subs)
            first[8 * q + j, q], first[8 * q + j + 1, q] = at, at + 8
            inner[8 * q + 6 - j, q] = at + j + 1
            if j == 0:
                inner[8 * q + 5, q] = at + 10
            subs.append(("mixed", 8 * q, j))
    for q in range(0, regress // 8, 2):
        first[8 * q + 7, q], first[8 * q + 15, q + 1] = 16 * len(subs), 16 * len(subs) + 8
        subs.append(("ends", 8 * q, 0))
    for a in range(0, regress, 2):
        blocks = a // 8
        for one in (a, a + 1):
            for m in range(blocks // 2):
                first[one, 2 * m] = 16 * len(subs)
                first[one, 2 * m + 1] = 16 * len(subs) + 8
                subs.append(("full", one, m))
        if blocks % 2:
            first[a, blocks - 1] = 16 * len(subs)
            first[a + 1, blocks - 1] = 16 * len(subs) + 8
            subs.append(("half", a, blocks - 1))
    return subs, first, inner


def packed_lanes(regress):
    at = 16 * len(pair_layout(regress)[0])
    return at, at + regress, at + 3 * regress


def row_groups(bits):
    return [(shift, min(2, bits - shift)) for shift in range(0, bits, 2)]


def place_of(bits, core, row):
    place = core
    for shift, count in row_groups(bits - 1):
        place = (place << count) | ((row >> shift) & ((1 << count) - 1))
    return place


def own_leaves(bits):
    return place_of(bits, lax.axis_index("leaf"), lax.axis_index("row")) * (LEAVES >> bits)


def add_tiles(subs, out_width, step, range_ref, feat_all, hess_all, grad_all, hot_all, keep_ref, send_ref, w_ref, before, after):
    regress, rows = feat_all.shape
    with_grad = subs[-1][0] == "grad_low"
    origin = (lax.axis_index("row") * 2 + lax.axis_index("leaf")) * rows

    def chunk(k, fresh):
        at = pl.ds(k * step if isinstance(k, int) else pl.multiple_of(k * step, step), step)
        before(k, at)
        position = origin + k * step + lax.broadcasted_iota(I32, (1, step), 1)
        inside = jnp.where((position >= range_ref[0]) & (position < range_ref[1]), 1.0, 0.0)
        hess = hess_all[:, at] * inside
        grad = (grad_all[:, at] * inside).astype(BF16)
        hess_b = hess.astype(BF16)
        hot = hot_all[:, at]
        feat = feat_all[:, at]
        feat_f = feat.astype(F32)
        w_ref[...] = feat_f * hess

        @functools.lru_cache(None)
        def weight(a, count):
            return jnp.broadcast_to(w_ref[a:a + 1, :], (count, step))

        @functools.lru_cache(None)
        def weight_b(a):
            return weight(a, 16).astype(BF16)

        @functools.lru_cache(None)
        def twice(m):
            part = feat_f[8 * m:8 * m + 8]
            return jnp.concatenate([part, part], 0).astype(BF16)

        def eight(q, j, pair):
            part = feat_f[8 * q:8 * q + 8]
            if not pair:
                return weight(8 * q + j, 8), part
            mine = lax.broadcasted_iota(I32, (8, step), 0) <= j
            moved = jnp.concatenate([part[7 - j:], part[:7 - j]], 0)
            return jnp.where(mine, weight(8 * q + j, 8), weight(8 * q + 6 - j, 8)), jnp.where(mine, part, moved)

        def join(one, other):
            return jnp.concatenate([one[0], other[0]], 0).astype(BF16) * jnp.concatenate([one[1], other[1]], 0).astype(BF16)

        def rows_of(sub):
            kind, a, m = sub
            if kind == "ends":
                return join(eight(a // 8, 7, False), eight(a // 8 + 1, 7, False))
            if kind == "mixed":
                tile = join(eight(a // 8, m, True), eight(a // 8, m + 1, m == 0))
                if a == 0 and m == 2:
                    row = 16 + lax.broadcasted_iota(I32, (16, step), 0)
                    tile_f = tile.astype(F32)
                    tile_f = jnp.where(row == HESS, hess_b.astype(F32), tile_f)
                    tile_f = jnp.where(row == GRAD, grad.astype(F32), tile_f)
                    tile = tile_f.astype(BF16)
                return tile
            if kind == "full":
                return weight_b(a) * feat[16 * m:16 * m + 16]
            if kind == "half":
                both = jnp.concatenate([weight(a, 8), weight(a + 1, 8)], 0).astype(BF16)
                return both * twice(m)
            if kind == "weight":
                return w_ref[16 * m:16 * m + 16, :].astype(BF16)
            exact = feat_f[16 * m:16 * m + 16] * grad.astype(F32)
            high = exact.astype(BF16)
            if kind == "grad_high":
                return high
            return (exact - high.astype(F32)).astype(BF16)

        for t in range(len(subs) * 16 // 256):
            tile = jnp.concatenate([rows_of(s) for s in subs[16 * t:16 * t + 16]], 0)
            part = lax.dot_general(hot, tile, NT, preferred_element_type=F32)
            if with_grad and (t + 1) * 256 == out_width:
                tail = part[:, 128:]
                part = jnp.concatenate([part[:, :128], tail + pltpu.roll(tail, 64, 1)], 1)
            lanes = slice(t * 256, t * 256 + 256)
            if fresh:
                keep_ref[:, lanes] = part[:LEAVES // 2]
                send_ref[:, lanes] = part[LEAVES // 2:]
            else:
                keep_ref[:, lanes] += part[:LEAVES // 2]
                send_ref[:, lanes] += part[LEAVES // 2:]
        after(hess_b.astype(F32), jnp.abs(grad.astype(F32)))

    chunk(0, True)
    if rows > step:
        lax.fori_loop(1, rows // step, lambda k, carry: (chunk(k, False), carry)[1], 0)


def first_kernel(subs, out_width, step, bits, range_ref, feat_hbm, hess_hbm, grad_hbm, leaf_hbm, keep_ref, send_ref, hot_all, feat_all, hess_all, grad_all, leaf_all, w_ref, total_ref, sems, feat_sems):
    rows = feat_all.shape[1]
    copies = [
        pltpu.make_async_copy(source, target, sems.at[i])
        for i, (source, target) in enumerate(((leaf_hbm, leaf_all), (hess_hbm, hess_all), (grad_hbm, grad_all)))
    ]

    def feat_copy(k):
        at = pl.ds(k * step if isinstance(k, int) else pl.multiple_of(k * step, step), step)
        return pltpu.make_async_copy(feat_hbm.at[:, at], feat_all.at[:, at], feat_sems.at[k])

    for copy in copies:
        copy.start()
    for k in range(rows // step):
        feat_copy(k).start()
    total_ref[...] = jnp.zeros_like(total_ref)
    for copy in copies:
        copy.wait()
    own = own_leaves(bits)

    def before(k, at):
        leaf = (leaf_all[:, at] ^ own).astype(F32).astype(BF16)
        names = lax.broadcasted_iota(I32, (LEAVES, 128), 0).astype(F32).astype(BF16)
        names = jnp.concatenate([names] * (step // 128), 1)
        hot_all[:, at] = jnp.where(names == leaf, jnp.ones((), BF16), jnp.zeros((), BF16))
        feat_copy(k).wait()

    def after(hess, grad):
        total_ref[0:1, :] += hess
        total_ref[1:2, :] += grad

    add_tiles(subs, out_width, step, range_ref, feat_all, hess_all, grad_all, hot_all, keep_ref, send_ref, w_ref, before, after)
    hess_total, grad_total = jnp.sum(total_ref[0:1, :]), jnp.sum(total_ref[1:2, :])
    lane = lax.broadcasted_iota(I32, (LEAVES // 2, 128), 1)
    for ref in (keep_ref, send_ref):
        first = jnp.where(lane == HESS_ALL, hess_total, ref[:, :128])
        ref[:, :128] = jnp.where(lane == GRAD_ALL, grad_total, first)


def later_kernel(subs, out_width, step, range_ref, hot_all, feat_all, hess_all, grad_all, keep_ref, send_ref, w_ref):
    nothing = lambda *ignored: None
    add_tiles(subs, out_width, step, range_ref, feat_all, hess_all, grad_all, hot_all, keep_ref, send_ref, w_ref, nothing, nothing)


def sums_cost(subs, out_width, rows):
    return pl.CostEstimate(flops=2 * LEAVES * rows * len(subs) * 16, bytes_accessed=rows * 656 + LEAVES * out_width * 4, transcendentals=0)


def first_call(subs, out_width, step, bits, train_range, features, hessian, gradient, leaf):
    regress, rows = features.shape
    return pl.pallas_call(
        functools.partial(first_kernel, subs, out_width, step, bits),
        in_specs=[pl.BlockSpec(memory_space=pltpu.SMEM)] + [pl.BlockSpec(memory_space=pltpu.HBM)] * 4,
        out_specs=[pl.BlockSpec(memory_space=pltpu.VMEM)] * 6,
        out_shape=[jax.ShapeDtypeStruct((LEAVES // 2, out_width), F32)] * 2
        + [jax.ShapeDtypeStruct((LEAVES, rows), BF16), jax.ShapeDtypeStruct((regress, rows), BF16)]
        + [jax.ShapeDtypeStruct((1, rows), F32)] * 2,
        scratch_shapes=[
            pltpu.VMEM((1, rows), I32),
            pltpu.VMEM((regress, step), F32),
            pltpu.VMEM((2, step), F32),
            pltpu.SemaphoreType.DMA((3,)),
            pltpu.SemaphoreType.DMA((rows // step,)),
        ],
        compiler_params=pltpu.CompilerParams(vmem_limit_bytes=28 << 20),
        cost_estimate=sums_cost(subs, out_width, rows),
    )(*[pltpu.with_memory_space_constraint(x, pltpu.HBM) for x in (train_range, features, hessian, gradient, leaf)])


def later_call(subs, out_width, step, train_range, hot, features, hessian, gradient):
    regress, rows = features.shape
    return pl.pallas_call(
        functools.partial(later_kernel, subs, out_width, step),
        in_specs=[pl.BlockSpec(memory_space=pltpu.SMEM)] + [pl.BlockSpec(memory_space=pltpu.VMEM)] * 4,
        out_specs=[pl.BlockSpec(memory_space=pltpu.VMEM)] * 2,
        out_shape=[jax.ShapeDtypeStruct((LEAVES // 2, out_width), F32)] * 2,
        scratch_shapes=[pltpu.VMEM((regress, step), F32)],
        compiler_params=pltpu.CompilerParams(vmem_limit_bytes=28 << 20),
        cost_estimate=sums_cost(subs, out_width, rows),
    )(train_range, hot, features, hessian, gradient)


def spread(regress, lane, hess, grad):
    if lane >= packed_lanes(regress)[1]:
        return grad
    if lane:
        return hess
    at = lax.broadcasted_iota(I32, hess.shape, 1)
    return jnp.where((at == GRAD) | (at == GRAD_ALL), grad, hess)


def carried_factors(ref):
    wide = (ref.shape[0], 128)
    return [jnp.broadcast_to(jnp.exp2(ref[:, at:at + 1]), wide) for at in (HESS_UNIT, GRAD_UNIT)]


def decoded(regress, lane, ref, factors):
    return ref[:, lane:lane + 128] * spread(regress, lane, *factors)


def solve_kernel(regress, mine_ref, other_ref, out_ref, t_ref, u_ref, z_ref, c_ref):
    held, lanes = mine_ref.shape
    last_at, grad_at, _ = packed_lanes(regress)
    _, first, inner = pair_layout(regress)
    factors = [carried_factors(ref) for ref in (mine_ref, other_ref)]
    for lane in range(0, lanes, 128):
        tile = decoded(regress, lane, mine_ref, factors[0]) + decoded(regress, lane, other_ref, factors[1])
        tile = jnp.concatenate([tile, jnp.zeros((128 - held, 128), F32)], 0)
        t_ref[lane:lane + 128, :] = tile.T
    first = dict(first)
    for (a, m), at in inner.items():
        first[a, m] = lanes + 8 * list(inner).index((a, m))
        t_ref[first[a, m]:first[a, m] + 8, :] = t_ref[at:at + 8, :]
    last = regress
    for m in range(regress // 8):
        first[last, m] = last_at + 8 * m
    real = lax.broadcasted_iota(I32, (1, 128), 1) < held
    ridge = jnp.where(real, t_ref[HESS_ALL:HESS_ALL + 1, :] * (0.5 / LEAVES), 1.0)
    blocks = regress // 8

    def row(a, m):
        return t_ref[first[a, m]:first[a, m] + 8, :]

    def pivot(a, own, count):
        inverse = 1.0 / (own + ridge)
        for m in range(count):
            u_ref[a, 8 * m:8 * m + 8, :] = row(a, m) * inverse
        return inverse

    def reduce_target(a, inverse, value):
        scaled = value * inverse
        z_ref[a:a + 1, :] = scaled
        for m in range((a + 7) // 8):
            t_ref[grad_at + 8 * m:grad_at + 8 * m + 8, :] -= row(a, m) * scaled

    for m in range(blocks):
        t_ref[grad_at + 8 * m:grad_at + 8 * m + 8, :] = -t_ref[grad_at + 8 * m:grad_at + 8 * m + 8, :]
    inverse = pivot(last, t_ref[HESS:HESS + 1, :], blocks)
    reduce_target(last, inverse, -t_ref[GRAD:GRAD + 1, :])
    for q in range(blocks - 1, -1, -1):
        for top in (8 * q + 4, 8 * q):
            some = range(top + 3, top - 1, -1)
            total = {(a, m): row(a, m) for a in some for m in range(q + 1)}
            for k in range(last, 8 * q + 7, -1):
                line = [row(k, m) for m in range(q + 1)]
                for a in some:
                    scale = u_ref[k, a:a + 1, :]
                    for m in range(q + 1):
                        total[a, m] = total[a, m] - scale * line[m]
            for (a, m), value in total.items():
                t_ref[first[a, m]:first[a, m] + 8, :] = value
        for a in range(8 * q + 7, 8 * q - 1, -1):
            total = [row(a, m) for m in range(q + 1)]
            for k in range(8 * q + 7, a, -1):
                scale = u_ref[k, a:a + 1, :]
                for m in range(q + 1):
                    total[m] = total[m] - scale * row(k, m)
            for m in range(q + 1):
                t_ref[first[a, m]:first[a, m] + 8, :] = total[m]
            at = first[a, q] + a % 8
            inverse = pivot(a, t_ref[at:at + 1, :], q + 1)
            reduce_target(a, inverse, t_ref[grad_at + a:grad_at + a + 1, :])
    c_ref[...] = jnp.zeros_like(c_ref)
    for q in range(blocks + 1):
        rows = range(8 * q, min(8 * q + 8, regress + 1))
        known = {}
        for k in rows:
            value = z_ref[k:k + 1, :]
            if q:
                products = u_ref[k, 0:8, :] * c_ref[0:8, :]
                for m in range(1, q):
                    products = products + u_ref[k, 8 * m:8 * m + 8, :] * c_ref[8 * m:8 * m + 8, :]
                value = value - jnp.sum(products, 0, keepdims=True)
            known[k] = value
        for k in rows:
            for b in range(8 * q, k):
                known[k] = known[k] - u_ref[k, b:b + 1, :] * known[b]
        for k in rows:
            c_ref[k:k + 1, :] = known[k]
    out_ref[...] = c_ref[...].T[:held]


def solve_call(regress, mine, other):
    held, lanes = mine.shape
    return pl.pallas_call(
        functools.partial(solve_kernel, regress),
        out_shape=jax.ShapeDtypeStruct((held, 128), F32),
        in_specs=[pl.BlockSpec(memory_space=pltpu.VMEM)] * 2,
        out_specs=pl.BlockSpec(memory_space=pltpu.VMEM),
        scratch_shapes=[
            pltpu.VMEM((lanes + 3 * regress, 128), F32),
            pltpu.VMEM((regress + 1, regress, 128), F32),
            pltpu.VMEM((72, 128), F32),
            pltpu.VMEM((128, 128), F32),
        ],
        compiler_params=pltpu.CompilerParams(vmem_limit_bytes=28 << 20),
    )(mine, other)


def apply_kernel(places, block, step, bits, *refs):
    part_refs = refs[:len(places)]
    hot_ref, feat_ref, hess_ref, grad_ref, coef_ref, next_ref, real_ref, own_ref = refs[len(places):]
    regress, rows = feat_ref.shape
    own = own_leaves(bits)
    for ref, owners in zip(part_refs, places):
        for at, place in enumerate(owners):
            value = ref[at * block:(at + 1) * block, :]
            own_ref[place * block:(place + 1) * block, :] = value
            real_ref[pl.ds(pl.multiple_of((place * block) ^ own, block), block), :] = value
    turned = own_ref[...].T[:80]
    high = turned.astype(BF16)
    both = jnp.concatenate([high, (turned - high.astype(F32)).astype(BF16)], 0)
    for start in range(0, rows, step):
        at = slice(start, start + step)
        picked = jnp.dot(both, hot_ref[:, at], preferred_element_type=F32)
        picked = picked[:80] + picked[80:]
        predicted = jnp.sum(picked[:regress] * feat_ref[:, at].astype(F32), 0, keepdims=True) + picked[regress:regress + 1]
        next_ref[:, at] = grad_ref[:, at] + hess_ref[:, at] * predicted
    coef_ref[...] = real_ref[...].T[:regress + 1]


def apply_call(places, block, parts, step, bits, hot, features, hessian, gradient):
    regress, rows = features.shape
    return pl.pallas_call(
        functools.partial(apply_kernel, places, block, step, bits),
        in_specs=[pl.BlockSpec(memory_space=pltpu.VMEM)] * (len(parts) + 4),
        out_specs=[pl.BlockSpec(memory_space=pltpu.VMEM)] * 2,
        out_shape=[jax.ShapeDtypeStruct((regress + 1, LEAVES), F32), jax.ShapeDtypeStruct((1, rows), F32)],
        scratch_shapes=[pltpu.VMEM((LEAVES, 128), F32), pltpu.VMEM((LEAVES, 128), F32)],
        compiler_params=pltpu.CompilerParams(vmem_limit_bytes=28 << 20),
    )(*parts, hot, features, hessian, gradient)


def combine_kernel(regress, plain, coded, size, starts, *refs):
    lanes = packed_lanes(regress)[2]
    pieces = len(starts)
    plain_refs, coded_refs, out_refs = refs[:plain * pieces], refs[plain * pieces:plain * pieces + coded], refs[plain * pieces + coded:]
    rows = plain_refs[0].shape[0]
    factors = [carried_factors(ref) for ref in coded_refs]

    def total(lane):
        piece = max(i for i in range(pieces) if starts[i] <= lane)
        at = lane - starts[piece]
        value = plain_refs[piece][:, at:at + 128]
        for p in range(1, plain):
            value = value + plain_refs[p * pieces + piece][:, at:at + 128]
        for ref, factor in zip(coded_refs, factors):
            value = value + decoded(regress, lane, ref, factor)
        return value

    head = total(0)
    hess_unit = jnp.clip(jnp.ceil(jnp.log2(head[:, HESS_ALL:HESS_ALL + 1] * (36.0 / 50000.0))), -100.0, 100.0)
    grad_unit = jnp.clip(jnp.ceil(jnp.log2(head[:, GRAD_ALL:GRAD_ALL + 1] * (6.0 / 50000.0))), -100.0, 100.0)
    own = [jnp.broadcast_to(jnp.exp2(-unit), (rows, 128)) for unit in (hess_unit, grad_unit)]
    for lane in range(0, lanes, 128):
        value = total(lane) if lane else head
        code = value * spread(regress, lane, *own)
        if lane == 0:
            at = lax.broadcasted_iota(I32, (rows, 128), 1)
            code = jnp.where(at == HESS_UNIT, hess_unit, jnp.where(at == GRAD_UNIT, grad_unit, code))
        if size:
            out_refs[1][:, lane:lane + 128] = value[:size]
        out_refs[0][:, lane:lane + 128] = code[size:]


def combine_call(regress, plain, coded, size):
    lanes = packed_lanes(regress)[2]
    rows = plain[0][0].shape[0]
    starts, at = [], 0
    for piece in plain[0]:
        starts.append(at)
        at += piece.shape[1]
    shapes = [jax.ShapeDtypeStruct((rows - size, lanes), F32)] + [jax.ShapeDtypeStruct((size, lanes), F32)] * (size > 0)
    operands = [piece for part in plain for piece in part] + [x.astype(F32) for x in coded]
    code, *own = pl.pallas_call(
        functools.partial(combine_kernel, regress, len(plain), len(coded), size, starts),
        in_specs=[pl.BlockSpec(memory_space=pltpu.VMEM)] * len(operands),
        out_specs=[pl.BlockSpec(memory_space=pltpu.VMEM)] * len(shapes),
        out_shape=shapes,
        compiler_params=pltpu.CompilerParams(vmem_limit_bytes=28 << 20),
    )(*operands)
    step = size or rows
    return [lax.optimization_barrier(code[at:at + step].astype(F16)) for at in range(0, rows - size, step)], own


def swap_rows(x, rows, distance):
    return lax.ppermute(x, "row", [(r, r ^ distance) for r in range(rows)])


def body(features, hessian, gradient, leaf_index, train_range):
    regress, local = features.shape
    rows = lax.axis_size("row")
    bits = rows.bit_length() - 1
    groups = row_groups(bits - 1)
    block = LEAVES >> bits
    subs = pair_layout(regress)[0]
    for kind in ("weight", "grad_high", "grad_low"):
        subs = subs + [(kind, 0, m) for m in range(regress // 16)]
    keeps, gots, shared = [], [], None
    for begin, end in CALLS:
        part = subs[16 * begin:16 * end]
        width = 256 * (end - begin)
        if shared is None:
            keep, send, *shared = first_call(part, width, FIRST_STEP, bits, train_range, features, hessian.reshape(1, local), gradient.reshape(1, local), leaf_index.reshape(1, local))
        else:
            train_range, _ = lax.optimization_barrier((train_range, send))
            keep, send = later_call(part, width, LATER_STEP, train_range, *shared)
        keeps.append(keep)
        gots.append(lax.ppermute(send, "leaf", [(0, 1), (1, 0)]))
    plain, coded, size = [keeps, gots], [], LEAVES // 2
    for shift, count in groups:
        size >>= count
        sent, own = combine_call(regress, plain, coded, size)
        plain, coded = [own], [swap_rows(x, rows, (d + 1) << shift) for d, x in enumerate(sent)]
    (mine,), _ = combine_call(regress, plain, coded, 0)
    both = [mine, swap_rows(mine, rows, rows // 2)]
    both = [jnp.pad(x.astype(F32), ((0, -block % 8), (0, 0))) for x in both]
    coef = solve_call(regress, *both)[:block]
    both = jnp.concatenate([coef, lax.ppermute(coef, "leaf", [(0, 1), (1, 0)])], 0)
    held = [([0], both)]
    for shift, count in groups:
        names = [d for owners, _ in held for d in owners]
        array = jnp.concatenate([x for _, x in held], 0) if len(held) > 1 else held[0][1]
        held = held + [([n ^ (d << shift) for n in names], swap_rows(array, rows, d << shift)) for d in range(1, 1 << count)]
    places = [[place_of(bits, c, d) for d in owners for c in range(2)] for owners, _ in held]
    coefficients, following = apply_call(places, block, [x for _, x in held], APPLY_STEP, bits, *shared)
    return coefficients.T, following.reshape(local)


def solution(mesh):
    placed = (
        P(None, ("fold", "row", "leaf")),
        P(("fold", "row", "leaf")),
        P(("fold", "row", "leaf")),
        P(("fold", "row", "leaf"), None),
        P("fold"),
    )
    return jax.shard_map(
        body,
        mesh=mesh,
        in_specs=placed,
        out_specs=(P("fold", None), P(("fold", "row", "leaf"))),
        check_vma=False,
    )
```

```python
import functools
import jax
import jax.numpy as jnp
from jax import lax
from jax.experimental import pallas as pl
from jax.experimental.pallas import tpu as pltpu
from jax.sharding import PartitionSpec as P

LEAVES = 256
FIRST_STEP, LATER_STEP, APPLY_STEP = 2048, 4096, 2048
CALLS = ((0, 8), (8, 9))
HESS, GRAD, HESS_ALL, GRAD_ALL, HESS_UNIT, GRAD_UNIT = 28, 29, 30, 31, 60, 61
F32, BF16, F16, I32 = jnp.float32, jnp.bfloat16, jnp.float16, jnp.int32
NT = (((1,), (1,)), ((), ()))


def pair_layout(regress):
    subs, first, inner = [], {}, {}

    def mixed(q):
        for j in (0, 2):
            at = 16 * len(subs)
            first[8 * q + j, q], first[8 * q + j + 1, q] = at, at + 8
            inner[8 * q + 6 - j, q] = at + j + 1
            if j == 0:
                inner[8 * q + 5, q] = at + 10
            subs.append(("mixed", 8 * q, j))

    mixed(0)
    mixed(1)
    for q in range(0, regress // 8, 2):
        first[8 * q + 7, q], first[8 * q + 15, q + 1] = 16 * len(subs), 16 * len(subs) + 8
        subs.append(("ends", 8 * q, 0))
    for a in range(0, regress, 2):
        blocks = a // 8
        if a % 8 == 0 and blocks > 1:
            mixed(blocks)
        for one in (a, a + 1):
            for m in range(blocks // 2):
                first[one, 2 * m] = 16 * len(subs)
                first[one, 2 * m + 1] = 16 * len(subs) + 8
                subs.append(("full", one, m))
        if blocks % 2:
            first[a, blocks - 1] = 16 * len(subs)
            first[a + 1, blocks - 1] = 16 * len(subs) + 8
            subs.append(("half", a, blocks - 1))
    return subs, first, inner


def packed_lanes(regress):
    at = 16 * len(pair_layout(regress)[0])
    return at, at + regress, at + 3 * regress


def row_groups(bits):
    return [(shift, min(2, bits - shift)) for shift in range(0, bits, 2)]


def place_of(bits, core, row):
    place = core
    for shift, count in row_groups(bits - 1):
        place = (place << count) | ((row >> shift) & ((1 << count) - 1))
    return place


def own_leaves(bits):
    return place_of(bits, lax.axis_index("leaf"), lax.axis_index("row")) * (LEAVES >> bits)


def add_tiles(subs, out_width, step, range_ref, feat_all, hess_all, grad_all, hot_all, keep_ref, send_ref, w_ref, before, after):
    regress, rows = feat_all.shape
    with_grad = subs[-1][0] == "grad_low"
    origin = (lax.axis_index("row") * 2 + lax.axis_index("leaf")) * rows

    def chunk(k, fresh):
        at = pl.ds(k * step if isinstance(k, int) else pl.multiple_of(k * step, step), step)
        before(k, at)
        position = origin + k * step + lax.broadcasted_iota(I32, (1, step), 1)
        inside = jnp.where((position >= range_ref[0]) & (position < range_ref[1]), 1.0, 0.0)
        hess = hess_all[:, at] * inside
        grad = (grad_all[:, at] * inside).astype(BF16)
        hess_b = hess.astype(BF16)
        hot = hot_all[:, at]
        feat = feat_all[:, at]
        feat_f = feat.astype(F32)
        w_ref[...] = feat_f * hess

        @functools.lru_cache(None)
        def weight(a, count):
            return jnp.broadcast_to(w_ref[a:a + 1, :], (count, step))

        @functools.lru_cache(None)
        def weight_b(a):
            return weight(a, 16).astype(BF16)

        @functools.lru_cache(None)
        def twice(m):
            part = feat_f[8 * m:8 * m + 8]
            return jnp.concatenate([part, part], 0).astype(BF16)

        def eight(q, j, pair):
            part = feat_f[8 * q:8 * q + 8]
            value = weight(8 * q + j, 8) * part
            if not pair:
                return value
            moved = jnp.concatenate([part[7 - j:], part[:7 - j]], 0)
            return jnp.where(lax.broadcasted_iota(I32, (8, step), 0) <= j, value, weight(8 * q + 6 - j, 8) * moved)

        def join(one, other):
            return jnp.concatenate([one, other], 0).astype(BF16)

        def rows_of(sub):
            kind, a, m = sub
            if kind == "ends":
                return join(eight(a // 8, 7, False), eight(a // 8 + 1, 7, False))
            if kind == "mixed":
                tile = join(eight(a // 8, m, True), eight(a // 8, m + 1, m == 0))
                if a == 0 and m == 2:
                    row = 16 + lax.broadcasted_iota(I32, (16, step), 0)
                    tile_f = tile.astype(F32)
                    tile_f = jnp.where(row == HESS, hess_b.astype(F32), tile_f)
                    tile_f = jnp.where(row == GRAD, grad.astype(F32), tile_f)
                    tile = tile_f.astype(BF16)
                return tile
            if kind == "full":
                return weight_b(a) * feat[16 * m:16 * m + 16]
            if kind == "half":
                both = jnp.concatenate([weight(a, 8), weight(a + 1, 8)], 0).astype(BF16)
                return both * twice(m)
            if kind == "weight":
                return w_ref[16 * m:16 * m + 16, :].astype(BF16)
            exact = feat_f[16 * m:16 * m + 16] * grad.astype(F32)
            high = exact.astype(BF16)
            if kind == "grad_high":
                return high
            return (exact - high.astype(F32)).astype(BF16)

        for t in range(len(subs) * 16 // 256):
            tile = jnp.concatenate([rows_of(s) for s in subs[16 * t:16 * t + 16]], 0)
            part = lax.dot_general(hot, tile, NT, preferred_element_type=F32)
            if with_grad and (t + 1) * 256 == out_width:
                tail = part[:, 128:]
                part = jnp.concatenate([part[:, :128], tail + pltpu.roll(tail, 64, 1)], 1)
            lanes = slice(t * 256, t * 256 + 256)
            if fresh:
                keep_ref[:, lanes] = part[:LEAVES // 2]
                send_ref[:, lanes] = part[LEAVES // 2:]
            else:
                keep_ref[:, lanes] += part[:LEAVES // 2]
                send_ref[:, lanes] += part[LEAVES // 2:]
        after(hess_b.astype(F32), jnp.abs(grad.astype(F32)))

    chunk(0, True)
    if rows > step:
        lax.fori_loop(1, rows // step, lambda k, carry: (chunk(k, False), carry)[1], 0)


def first_kernel(subs, out_width, step, bits, range_ref, feat_hbm, hess_hbm, grad_hbm, leaf_hbm, keep_ref, send_ref, hot_all, feat_all, hess_all, grad_all, leaf_all, w_ref, total_ref, sems, feat_sems):
    rows = feat_all.shape[1]
    copies = [
        pltpu.make_async_copy(source, target, sems.at[i])
        for i, (source, target) in enumerate(((leaf_hbm, leaf_all), (hess_hbm, hess_all), (grad_hbm, grad_all)))
    ]

    def feat_copy(k):
        at = pl.ds(k * step if isinstance(k, int) else pl.multiple_of(k * step, step), step)
        return pltpu.make_async_copy(feat_hbm.at[:, at], feat_all.at[:, at], feat_sems.at[k])

    for copy in copies:
        copy.start()
    for k in range(rows // step):
        feat_copy(k).start()
    total_ref[...] = jnp.zeros_like(total_ref)
    for copy in copies:
        copy.wait()
    own = own_leaves(bits)

    def before(k, at):
        leaf = (leaf_all[:, at] ^ own).astype(F32).astype(BF16)
        names = lax.broadcasted_iota(I32, (LEAVES, 128), 0).astype(F32).astype(BF16)
        names = jnp.concatenate([names] * (step // 128), 1)
        hot_all[:, at] = jnp.where(names == leaf, jnp.ones((), BF16), jnp.zeros((), BF16))
        feat_copy(k).wait()

    def after(hess, grad):
        total_ref[0:1, :] += hess
        total_ref[1:2, :] += grad

    add_tiles(subs, out_width, step, range_ref, feat_all, hess_all, grad_all, hot_all, keep_ref, send_ref, w_ref, before, after)
    hess_total, grad_total = jnp.sum(total_ref[0:1, :]), jnp.sum(total_ref[1:2, :])
    lane = lax.broadcasted_iota(I32, (LEAVES // 2, 128), 1)
    for ref in (keep_ref, send_ref):
        first = jnp.where(lane == HESS_ALL, hess_total, ref[:, :128])
        ref[:, :128] = jnp.where(lane == GRAD_ALL, grad_total, first)


def later_kernel(subs, out_width, step, range_ref, hot_all, feat_all, hess_all, grad_all, keep_ref, send_ref, w_ref):
    nothing = lambda *ignored: None
    add_tiles(subs, out_width, step, range_ref, feat_all, hess_all, grad_all, hot_all, keep_ref, send_ref, w_ref, nothing, nothing)


def sums_cost(subs, out_width, rows):
    return pl.CostEstimate(flops=2 * LEAVES * rows * len(subs) * 16, bytes_accessed=rows * 656 + LEAVES * out_width * 4, transcendentals=0)


def first_call(subs, out_width, step, bits, train_range, features, hessian, gradient, leaf):
    regress, rows = features.shape
    return pl.pallas_call(
        functools.partial(first_kernel, subs, out_width, step, bits),
        in_specs=[pl.BlockSpec(memory_space=pltpu.SMEM)] + [pl.BlockSpec(memory_space=pltpu.HBM)] * 4,
        out_specs=[pl.BlockSpec(memory_space=pltpu.VMEM)] * 6,
        out_shape=[jax.ShapeDtypeStruct((LEAVES // 2, out_width), F32)] * 2
        + [jax.ShapeDtypeStruct((LEAVES, rows), BF16), jax.ShapeDtypeStruct((regress, rows), BF16)]
        + [jax.ShapeDtypeStruct((1, rows), F32)] * 2,
        scratch_shapes=[
            pltpu.VMEM((1, rows), I32),
            pltpu.VMEM((regress, step), F32),
            pltpu.VMEM((2, step), F32),
            pltpu.SemaphoreType.DMA((3,)),
            pltpu.SemaphoreType.DMA((rows // step,)),
        ],
        compiler_params=pltpu.CompilerParams(vmem_limit_bytes=28 << 20),
        cost_estimate=sums_cost(subs, out_width, rows),
    )(*[pltpu.with_memory_space_constraint(x, pltpu.HBM) for x in (train_range, features, hessian, gradient, leaf)])


def later_call(subs, out_width, step, train_range, hot, features, hessian, gradient):
    regress, rows = features.shape
    return pl.pallas_call(
        functools.partial(later_kernel, subs, out_width, step),
        in_specs=[pl.BlockSpec(memory_space=pltpu.SMEM)] + [pl.BlockSpec(memory_space=pltpu.VMEM)] * 4,
        out_specs=[pl.BlockSpec(memory_space=pltpu.VMEM)] * 2,
        out_shape=[jax.ShapeDtypeStruct((LEAVES // 2, out_width), F32)] * 2,
        scratch_shapes=[pltpu.VMEM((regress, step), F32)],
        compiler_params=pltpu.CompilerParams(vmem_limit_bytes=28 << 20),
        cost_estimate=sums_cost(subs, out_width, rows),
    )(train_range, hot, features, hessian, gradient)


def spread(regress, lane, hess, grad):
    if lane >= packed_lanes(regress)[1]:
        return grad
    if lane:
        return hess
    at = lax.broadcasted_iota(I32, hess.shape, 1)
    return jnp.where((at == GRAD) | (at == GRAD_ALL), grad, hess)


def carried_factors(ref):
    wide = (ref.shape[0], 128)
    return [jnp.broadcast_to(jnp.exp2(ref[:, at:at + 1]), wide) for at in (HESS_UNIT, GRAD_UNIT)]


def decoded(regress, lane, ref, factors):
    return ref[:, lane:lane + 128] * spread(regress, lane, *factors)


def solve_kernel(regress, mine_ref, other_ref, out_ref, t_ref, u_ref, z_ref, c_ref):
    held, lanes = mine_ref.shape
    last_at, grad_at, _ = packed_lanes(regress)
    _, first, inner = pair_layout(regress)
    factors = [carried_factors(ref) for ref in (mine_ref, other_ref)]
    for lane in range(0, lanes, 128):
        tile = decoded(regress, lane, mine_ref, factors[0]) + decoded(regress, lane, other_ref, factors[1])
        tile = jnp.concatenate([tile, jnp.zeros((128 - held, 128), F32)], 0)
        t_ref[lane:lane + 128, :] = tile.T
    first = dict(first)
    for (a, m), at in inner.items():
        first[a, m] = lanes + 8 * list(inner).index((a, m))
        t_ref[first[a, m]:first[a, m] + 8, :] = t_ref[at:at + 8, :]
    last = regress
    for m in range(regress // 8):
        first[last, m] = last_at + 8 * m
    real = lax.broadcasted_iota(I32, (1, 128), 1) < held
    ridge = jnp.where(real, t_ref[HESS_ALL:HESS_ALL + 1, :] * (0.5 / LEAVES), 1.0)
    blocks = regress // 8

    def row(a, m):
        return t_ref[first[a, m]:first[a, m] + 8, :]

    def pivot(a, own, count):
        inverse = 1.0 / (own + ridge)
        for m in range(count):
            u_ref[a, 8 * m:8 * m + 8, :] = row(a, m) * inverse
        return inverse

    def reduce_target(a, inverse, value):
        scaled = value * inverse
        z_ref[a:a + 1, :] = scaled
        for m in range((a + 7) // 8):
            t_ref[grad_at + 8 * m:grad_at + 8 * m + 8, :] -= row(a, m) * scaled

    for m in range(blocks):
        t_ref[grad_at + 8 * m:grad_at + 8 * m + 8, :] = -t_ref[grad_at + 8 * m:grad_at + 8 * m + 8, :]
    inverse = pivot(last, t_ref[HESS:HESS + 1, :], blocks)
    reduce_target(last, inverse, -t_ref[GRAD:GRAD + 1, :])
    for q in range(blocks - 1, -1, -1):
        for top in (8 * q + 4, 8 * q):
            some = range(top + 3, top - 1, -1)
            total = {(a, m): row(a, m) for a in some for m in range(q + 1)}
            for k in range(last, 8 * q + 7, -1):
                line = [row(k, m) for m in range(q + 1)]
                for a in some:
                    scale = u_ref[k, a:a + 1, :]
                    for m in range(q + 1):
                        total[a, m] = total[a, m] - scale * line[m]
            for (a, m), value in total.items():
                t_ref[first[a, m]:first[a, m] + 8, :] = value
        for a in range(8 * q + 7, 8 * q - 1, -1):
            total = [row(a, m) for m in range(q + 1)]
            for k in range(8 * q + 7, a, -1):
                scale = u_ref[k, a:a + 1, :]
                for m in range(q + 1):
                    total[m] = total[m] - scale * row(k, m)
            for m in range(q + 1):
                t_ref[first[a, m]:first[a, m] + 8, :] = total[m]
            at = first[a, q] + a % 8
            inverse = pivot(a, t_ref[at:at + 1, :], q + 1)
            reduce_target(a, inverse, t_ref[grad_at + a:grad_at + a + 1, :])
    c_ref[...] = jnp.zeros_like(c_ref)
    for q in range(blocks + 1):
        rows = range(8 * q, min(8 * q + 8, regress + 1))
        known = {}
        for k in rows:
            value = z_ref[k:k + 1, :]
            if q:
                products = u_ref[k, 0:8, :] * c_ref[0:8, :]
                for m in range(1, q):
                    products = products + u_ref[k, 8 * m:8 * m + 8, :] * c_ref[8 * m:8 * m + 8, :]
                value = value - jnp.sum(products, 0, keepdims=True)
            known[k] = value
        for k in rows:
            for b in range(8 * q, k):
                known[k] = known[k] - u_ref[k, b:b + 1, :] * known[b]
        for k in rows:
            c_ref[k:k + 1, :] = known[k]
    out_ref[...] = c_ref[...].T[:held]


def solve_call(regress, mine, other):
    held, lanes = mine.shape
    return pl.pallas_call(
        functools.partial(solve_kernel, regress),
        out_shape=jax.ShapeDtypeStruct((held, 128), F32),
        in_specs=[pl.BlockSpec(memory_space=pltpu.VMEM)] * 2,
        out_specs=pl.BlockSpec(memory_space=pltpu.VMEM),
        scratch_shapes=[
            pltpu.VMEM((lanes + 3 * regress, 128), F32),
            pltpu.VMEM((regress + 1, regress, 128), F32),
            pltpu.VMEM((72, 128), F32),
            pltpu.VMEM((128, 128), F32),
        ],
        compiler_params=pltpu.CompilerParams(vmem_limit_bytes=28 << 20),
    )(mine, other)


def apply_kernel(places, block, step, bits, *refs):
    part_refs = refs[:len(places)]
    hot_ref, feat_ref, hess_ref, grad_ref, coef_ref, next_ref, real_ref, own_ref = refs[len(places):]
    regress, rows = feat_ref.shape
    own = own_leaves(bits)
    for ref, owners in zip(part_refs, places):
        for at, place in enumerate(owners):
            value = ref[at * block:(at + 1) * block, :]
            own_ref[place * block:(place + 1) * block, :] = value
            real_ref[pl.ds(pl.multiple_of((place * block) ^ own, block), block), :] = value
    turned = own_ref[...].T[:80]
    high = turned.astype(BF16)
    both = jnp.concatenate([high, (turned - high.astype(F32)).astype(BF16)], 0)
    for start in range(0, rows, step):
        at = slice(start, start + step)
        picked = jnp.dot(both, hot_ref[:, at], preferred_element_type=F32)
        picked = picked[:80] + picked[80:]
        predicted = jnp.sum(picked[:regress] * feat_ref[:, at].astype(F32), 0, keepdims=True) + picked[regress:regress + 1]
        next_ref[:, at] = grad_ref[:, at] + hess_ref[:, at] * predicted
    coef_ref[...] = real_ref[...].T[:regress + 1]


def apply_call(places, block, parts, step, bits, hot, features, hessian, gradient):
    regress, rows = features.shape
    return pl.pallas_call(
        functools.partial(apply_kernel, places, block, step, bits),
        in_specs=[pl.BlockSpec(memory_space=pltpu.VMEM)] * (len(parts) + 4),
        out_specs=[pl.BlockSpec(memory_space=pltpu.VMEM)] * 2,
        out_shape=[jax.ShapeDtypeStruct((regress + 1, LEAVES), F32), jax.ShapeDtypeStruct((1, rows), F32)],
        scratch_shapes=[pltpu.VMEM((LEAVES, 128), F32), pltpu.VMEM((LEAVES, 128), F32)],
        compiler_params=pltpu.CompilerParams(vmem_limit_bytes=28 << 20),
    )(*parts, hot, features, hessian, gradient)


def combine_kernel(regress, plain, coded, size, starts, *refs):
    lanes = packed_lanes(regress)[2]
    pieces = len(starts)
    plain_refs, coded_refs, out_refs = refs[:plain * pieces], refs[plain * pieces:plain * pieces + coded], refs[plain * pieces + coded:]
    rows = plain_refs[0].shape[0]
    factors = [carried_factors(ref) for ref in coded_refs]

    def total(lane):
        piece = max(i for i in range(pieces) if starts[i] <= lane)
        at = lane - starts[piece]
        value = plain_refs[piece][:, at:at + 128]
        for p in range(1, plain):
            value = value + plain_refs[p * pieces + piece][:, at:at + 128]
        for ref, factor in zip(coded_refs, factors):
            value = value + decoded(regress, lane, ref, factor)
        return value

    head = total(0)
    hess_unit = jnp.clip(jnp.ceil(jnp.log2(head[:, HESS_ALL:HESS_ALL + 1] * (36.0 / 50000.0))), -100.0, 100.0)
    grad_unit = jnp.clip(jnp.ceil(jnp.log2(head[:, GRAD_ALL:GRAD_ALL + 1] * (6.0 / 50000.0))), -100.0, 100.0)
    own = [jnp.broadcast_to(jnp.exp2(-unit), (rows, 128)) for unit in (hess_unit, grad_unit)]
    for lane in range(0, lanes, 128):
        value = total(lane) if lane else head
        code = value * spread(regress, lane, *own)
        if lane == 0:
            at = lax.broadcasted_iota(I32, (rows, 128), 1)
            code = jnp.where(at == HESS_UNIT, hess_unit, jnp.where(at == GRAD_UNIT, grad_unit, code))
        if size:
            out_refs[1][:, lane:lane + 128] = value[:size]
        out_refs[0][:, lane:lane + 128] = code[size:]


def combine_call(regress, plain, coded, size):
    lanes = packed_lanes(regress)[2]
    rows = plain[0][0].shape[0]
    starts, at = [], 0
    for piece in plain[0]:
        starts.append(at)
        at += piece.shape[1]
    shapes = [jax.ShapeDtypeStruct((rows - size, lanes), F32)] + [jax.ShapeDtypeStruct((size, lanes), F32)] * (size > 0)
    operands = [piece for part in plain for piece in part] + [x.astype(F32) for x in coded]
    code, *own = pl.pallas_call(
        functools.partial(combine_kernel, regress, len(plain), len(coded), size, starts),
        in_specs=[pl.BlockSpec(memory_space=pltpu.VMEM)] * len(operands),
        out_specs=[pl.BlockSpec(memory_space=pltpu.VMEM)] * len(shapes),
        out_shape=shapes,
        compiler_params=pltpu.CompilerParams(vmem_limit_bytes=28 << 20),
    )(*operands)
    step = size or rows
    return [lax.optimization_barrier(code[at:at + step].astype(F16)) for at in range(0, rows - size, step)], own


def swap_rows(x, rows, distance):
    return lax.ppermute(x, "row", [(r, r ^ distance) for r in range(rows)])


def body(features, hessian, gradient, leaf_index, train_range):
    regress, local = features.shape
    rows = lax.axis_size("row")
    bits = rows.bit_length() - 1
    groups = row_groups(bits - 1)
    block = LEAVES >> bits
    subs = pair_layout(regress)[0]
    for kind in ("weight", "grad_high", "grad_low"):
        subs = subs + [(kind, 0, m) for m in range(regress // 16)]
    keeps, gots, shared = [], [], None
    for begin, end in CALLS:
        part = subs[16 * begin:16 * end]
        width = 256 * (end - begin)
        if shared is None:
            keep, send, *shared = first_call(part, width, FIRST_STEP, bits, train_range, features, hessian.reshape(1, local), gradient.reshape(1, local), leaf_index.reshape(1, local))
        else:
            train_range, _ = lax.optimization_barrier((train_range, send))
            keep, send = later_call(part, width, LATER_STEP, train_range, *shared)
        keeps.append(keep)
        gots.append(lax.ppermute(send, "leaf", [(0, 1), (1, 0)]))
    plain, coded, size = [keeps, gots], [], LEAVES // 2
    for shift, count in groups:
        size >>= count
        sent, own = combine_call(regress, plain, coded, size)
        plain, coded = [own], [swap_rows(sent[d - 1], rows, d << shift) for d in sorted(range(1, 1 << count), key=(3, 1, 2).index)]
    (mine,), _ = combine_call(regress, plain, coded, 0)
    both = [mine, swap_rows(mine, rows, rows // 2)]
    both = [jnp.pad(x.astype(F32), ((0, -block % 8), (0, 0))) for x in both]
    coef = solve_call(regress, *both)[:block]
    both = jnp.concatenate([coef, lax.ppermute(coef, "leaf", [(0, 1), (1, 0)])], 0)
    held = [([0], both)]
    for shift, count in groups:
        names = [d for owners, _ in held for d in owners]
        array = jnp.concatenate([x for _, x in held], 0) if len(held) > 1 else held[0][1]
        held = held + [([n ^ (d << shift) for n in names], swap_rows(array, rows, d << shift)) for d in range(1, 1 << count)]
    places = [[place_of(bits, c, d) for d in owners for c in range(2)] for owners, _ in held]
    coefficients, following = apply_call(places, block, [x for _, x in held], APPLY_STEP, bits, *shared)
    return coefficients.T, following.reshape(local)


def solution(mesh):
    placed = (
        P(None, ("fold", "row", "leaf")),
        P(("fold", "row", "leaf")),
        P(("fold", "row", "leaf")),
        P(("fold", "row", "leaf"), None),
        P("fold"),
    )
    return jax.shard_map(
        body,
        mesh=mesh,
        in_specs=placed,
        out_specs=(P("fold", None), P(("fold", "row", "leaf"))),
        check_vma=False,
    )
```

```python
import functools
import jax
import jax.numpy as jnp
from jax import lax
from jax.experimental import pallas as pl
from jax.experimental.pallas import tpu as pltpu
from jax.sharding import PartitionSpec as P

LEAVES = 256
FIRST_STEP, LATER_STEP, APPLY_STEP = 2048, 4096, 2048
CALLS = ((0, 8), (8, 9))
HESS, GRAD, HESS_ALL, GRAD_ALL, HESS_UNIT, GRAD_UNIT = 28, 29, 30, 31, 60, 61
F32, BF16, F16, I32 = jnp.float32, jnp.bfloat16, jnp.float16, jnp.int32
NT = (((1,), (1,)), ((), ()))


def pair_layout(regress):
    subs, first, inner = [], {}, {}

    def mixed(q):
        for j in (0, 2):
            at = 16 * len(subs)
            first[8 * q + j, q], first[8 * q + j + 1, q] = at, at + 8
            inner[8 * q + 6 - j, q] = at + j + 1
            if j == 0:
                inner[8 * q + 5, q] = at + 10
            subs.append(("mixed", 8 * q, j))

    mixed(0)
    mixed(1)
    for q in range(0, regress // 8, 2):
        first[8 * q + 7, q], first[8 * q + 15, q + 1] = 16 * len(subs), 16 * len(subs) + 8
        subs.append(("ends", 8 * q, 0))
    for a in range(0, regress, 2):
        blocks = a // 8
        if a % 8 == 0 and blocks > 1:
            mixed(blocks)
        for one in (a, a + 1):
            for m in range(blocks // 2):
                first[one, 2 * m] = 16 * len(subs)
                first[one, 2 * m + 1] = 16 * len(subs) + 8
                subs.append(("full", one, m))
        if blocks % 2:
            first[a, blocks - 1] = 16 * len(subs)
            first[a + 1, blocks - 1] = 16 * len(subs) + 8
            subs.append(("half", a, blocks - 1))
    return subs, first, inner


def packed_lanes(regress):
    at = 16 * len(pair_layout(regress)[0])
    return at, at + regress, at + 3 * regress


def row_groups(bits):
    return [(shift, min(2, bits - shift)) for shift in range(0, bits, 2)]


def place_of(bits, core, row):
    place = core
    for shift, count in row_groups(bits - 1):
        place = (place << count) | ((row >> shift) & ((1 << count) - 1))
    return place


def own_leaves(bits):
    return place_of(bits, lax.axis_index("leaf"), lax.axis_index("row")) * (LEAVES >> bits)


def add_tiles(subs, out_width, step, feat_all, hess_all, grad_all, hot_all, keep_ref, send_ref, w_ref, before):
    regress, rows = feat_all.shape
    with_grad = subs[-1][0] == "grad_low"

    def chunk(k, fresh):
        at = pl.ds(k * step if isinstance(k, int) else pl.multiple_of(k * step, step), step)
        before(k, at)
        hess = hess_all[:, at]
        grad = grad_all[:, at].astype(BF16)
        hess_b = hess.astype(BF16)
        hot = hot_all[:, at]
        feat = feat_all[:, at]
        feat_f = feat.astype(F32)
        w_ref[...] = feat_f * hess

        @functools.lru_cache(None)
        def weight(a, count):
            return jnp.broadcast_to(w_ref[a:a + 1, :], (count, step))

        @functools.lru_cache(None)
        def weight_b(a):
            return weight(a, 16).astype(BF16)

        @functools.lru_cache(None)
        def twice(m):
            part = feat_f[8 * m:8 * m + 8]
            return jnp.concatenate([part, part], 0).astype(BF16)

        def eight(q, j, pair):
            part = feat_f[8 * q:8 * q + 8]
            value = weight(8 * q + j, 8) * part
            if not pair:
                return value
            moved = jnp.concatenate([part[7 - j:], part[:7 - j]], 0)
            return jnp.where(lax.broadcasted_iota(I32, (8, step), 0) <= j, value, weight(8 * q + 6 - j, 8) * moved)

        def join(one, other):
            return jnp.concatenate([one, other], 0).astype(BF16)

        def rows_of(sub):
            kind, a, m = sub
            if kind == "ends":
                return join(eight(a // 8, 7, False), eight(a // 8 + 1, 7, False))
            if kind == "mixed":
                tile = join(eight(a // 8, m, True), eight(a // 8, m + 1, m == 0))
                if a == 0 and m == 2:
                    row = 16 + lax.broadcasted_iota(I32, (16, step), 0)
                    tile_f = tile.astype(F32)
                    tile_f = jnp.where(row == HESS, hess_b.astype(F32), tile_f)
                    tile_f = jnp.where(row == GRAD, grad.astype(F32), tile_f)
                    tile = tile_f.astype(BF16)
                return tile
            if kind == "full":
                return weight_b(a) * feat[16 * m:16 * m + 16]
            if kind == "half":
                both = jnp.concatenate([weight(a, 8), weight(a + 1, 8)], 0).astype(BF16)
                return both * twice(m)
            if kind == "weight":
                return w_ref[16 * m:16 * m + 16, :].astype(BF16)
            exact = feat_f[16 * m:16 * m + 16] * grad.astype(F32)
            high = exact.astype(BF16)
            if kind == "grad_high":
                return high
            return (exact - high.astype(F32)).astype(BF16)

        for t in range(len(subs) * 16 // 256):
            tile = jnp.concatenate([rows_of(s) for s in subs[16 * t:16 * t + 16]], 0)
            part = lax.dot_general(hot, tile, NT, preferred_element_type=F32)
            if with_grad and (t + 1) * 256 == out_width:
                tail = part[:, 128:]
                part = jnp.concatenate([part[:, :128], tail + pltpu.roll(tail, 64, 1)], 1)
            lanes = slice(t * 256, t * 256 + 256)
            if fresh:
                keep_ref[:, lanes] = part[:LEAVES // 2]
                send_ref[:, lanes] = part[LEAVES // 2:]
            else:
                keep_ref[:, lanes] += part[:LEAVES // 2]
                send_ref[:, lanes] += part[LEAVES // 2:]

    chunk(0, True)
    if rows > step:
        lax.fori_loop(1, rows // step, lambda k, carry: (chunk(k, False), carry)[1], 0)


def first_kernel(subs, out_width, step, bits, range_hbm, feat_hbm, hess_hbm, grad_hbm, leaf_hbm, keep_ref, send_ref, hot_all, feat_all, hess_all, grad_all, hess_in, grad_in, leaf_all, range_ref, w_ref, total_ref, sems, feat_sems):
    rows = feat_all.shape[1]
    copies = [
        pltpu.make_async_copy(source, target, sems.at[i])
        for i, (source, target) in enumerate(((leaf_hbm, leaf_all), (range_hbm, range_ref), (hess_hbm, hess_all), (grad_hbm, grad_all)))
    ]

    def feat_copy(k):
        at = pl.ds(k * step if isinstance(k, int) else pl.multiple_of(k * step, step), step)
        return pltpu.make_async_copy(feat_hbm.at[:, at], feat_all.at[:, at], feat_sems.at[k])

    for copy in copies:
        copy.start()
    for k in range(rows // step):
        feat_copy(k).start()
    own = own_leaves(bits)
    names = lax.broadcasted_iota(I32, (LEAVES, 128), 0).astype(F32).astype(BF16)
    names = jnp.concatenate([names] * (step // 128), 1)
    copies[0].wait()
    for k in range(rows // step):
        at = slice(k * step, (k + 1) * step)
        leaf = (leaf_all[:, at] ^ own).astype(F32).astype(BF16)
        hot_all[:, at] = jnp.where(names == leaf, jnp.ones((), BF16), jnp.zeros((), BF16))
    for copy in copies[1:]:
        copy.wait()
    origin = (lax.axis_index("row") * 2 + lax.axis_index("leaf")) * rows
    position = origin + lax.broadcasted_iota(I32, (1, rows), 1)
    inside = jnp.where((position >= range_ref[0]) & (position < range_ref[1]), 1.0, 0.0)
    hess_in[...] = hess_all[...] * inside
    grad_in[...] = grad_all[...] * inside
    hess_total = jnp.sum(hess_in[...].astype(BF16).astype(F32), 1, keepdims=True)
    grad_total = jnp.sum(jnp.abs(grad_in[...].astype(BF16).astype(F32)), 1, keepdims=True)
    total_ref[0:1, :] = jnp.broadcast_to(hess_total, (1, 128))
    total_ref[1:2, :] = jnp.broadcast_to(grad_total, (1, 128))

    def before(k, at):
        feat_copy(k).wait()

    add_tiles(subs, out_width, step, feat_all, hess_in, grad_in, hot_all, keep_ref, send_ref, w_ref, before)
    lane = lax.broadcasted_iota(I32, (LEAVES // 2, 128), 1)
    for ref in (keep_ref, send_ref):
        first = jnp.where(lane == HESS_ALL, total_ref[0:1, :], ref[:, :128])
        ref[:, :128] = jnp.where(lane == GRAD_ALL, total_ref[1:2, :], first)


def later_kernel(subs, out_width, step, hot_all, feat_all, hess_in, grad_in, keep_ref, send_ref, w_ref):
    add_tiles(subs, out_width, step, feat_all, hess_in, grad_in, hot_all, keep_ref, send_ref, w_ref, lambda k, at: None)


def sums_cost(subs, out_width, rows):
    return pl.CostEstimate(flops=2 * LEAVES * rows * len(subs) * 16, bytes_accessed=rows * 656 + LEAVES * out_width * 4, transcendentals=0)


def first_call(subs, out_width, step, bits, train_range, features, hessian, gradient, leaf):
    regress, rows = features.shape
    return pl.pallas_call(
        functools.partial(first_kernel, subs, out_width, step, bits),
        in_specs=[pl.BlockSpec(memory_space=pltpu.HBM)] * 5,
        out_specs=[pl.BlockSpec(memory_space=pltpu.VMEM)] * 8,
        out_shape=[jax.ShapeDtypeStruct((LEAVES // 2, out_width), F32)] * 2
        + [jax.ShapeDtypeStruct((LEAVES, rows), BF16), jax.ShapeDtypeStruct((regress, rows), BF16)]
        + [jax.ShapeDtypeStruct((1, rows), F32)] * 4,
        scratch_shapes=[
            pltpu.VMEM((1, rows), I32),
            pltpu.SMEM((2,), I32),
            pltpu.VMEM((regress, step), F32),
            pltpu.VMEM((2, 128), F32),
            pltpu.SemaphoreType.DMA((4,)),
            pltpu.SemaphoreType.DMA((rows // step,)),
        ],
        compiler_params=pltpu.CompilerParams(vmem_limit_bytes=28 << 20),
        cost_estimate=sums_cost(subs, out_width, rows),
    )(*[pltpu.with_memory_space_constraint(x, pltpu.HBM) for x in (train_range, features, hessian, gradient, leaf)])


def later_call(subs, out_width, step, hot, features, hessian, gradient):
    regress, rows = features.shape
    return pl.pallas_call(
        functools.partial(later_kernel, subs, out_width, step),
        in_specs=[pl.BlockSpec(memory_space=pltpu.VMEM)] * 4,
        out_specs=[pl.BlockSpec(memory_space=pltpu.VMEM)] * 2,
        out_shape=[jax.ShapeDtypeStruct((LEAVES // 2, out_width), F32)] * 2,
        scratch_shapes=[pltpu.VMEM((regress, step), F32)],
        compiler_params=pltpu.CompilerParams(vmem_limit_bytes=28 << 20),
        cost_estimate=sums_cost(subs, out_width, rows),
    )(hot, features, hessian, gradient)


def spread(regress, lane, hess, grad):
    if lane >= packed_lanes(regress)[1]:
        return grad
    if lane:
        return hess
    at = lax.broadcasted_iota(I32, hess.shape, 1)
    return jnp.where((at == GRAD) | (at == GRAD_ALL), grad, hess)


def carried_factors(ref):
    wide = (ref.shape[0], 128)
    return [jnp.broadcast_to(jnp.exp2(ref[:, at:at + 1]), wide) for at in (HESS_UNIT, GRAD_UNIT)]


def decoded(regress, lane, ref, factors):
    return ref[:, lane:lane + 128] * spread(regress, lane, *factors)


def solve_kernel(regress, mine_ref, other_ref, out_ref, t_ref, u_ref, z_ref, c_ref):
    held, lanes = mine_ref.shape
    last_at, grad_at, _ = packed_lanes(regress)
    _, first, inner = pair_layout(regress)
    factors = [carried_factors(ref) for ref in (mine_ref, other_ref)]
    for lane in range(0, lanes, 128):
        tile = decoded(regress, lane, mine_ref, factors[0]) + decoded(regress, lane, other_ref, factors[1])
        tile = jnp.concatenate([tile, jnp.zeros((128 - held, 128), F32)], 0)
        t_ref[lane:lane + 128, :] = tile.T
    first = dict(first)
    for (a, m), at in inner.items():
        first[a, m] = lanes + 8 * list(inner).index((a, m))
        t_ref[first[a, m]:first[a, m] + 8, :] = t_ref[at:at + 8, :]
    last = regress
    for m in range(regress // 8):
        first[last, m] = last_at + 8 * m
    real = lax.broadcasted_iota(I32, (1, 128), 1) < held
    ridge = jnp.where(real, t_ref[HESS_ALL:HESS_ALL + 1, :] * (0.5 / LEAVES), 1.0)
    blocks = regress // 8

    def row(a, m):
        return t_ref[first[a, m]:first[a, m] + 8, :]

    def pivot(a, own, count):
        inverse = 1.0 / (own + ridge)
        for m in range(count):
            u_ref[a, 8 * m:8 * m + 8, :] = row(a, m) * inverse
        return inverse

    def reduce_target(a, inverse, value):
        scaled = value * inverse
        z_ref[a:a + 1, :] = scaled
        for m in range((a + 7) // 8):
            t_ref[grad_at + 8 * m:grad_at + 8 * m + 8, :] -= row(a, m) * scaled

    for m in range(blocks):
        t_ref[grad_at + 8 * m:grad_at + 8 * m + 8, :] = -t_ref[grad_at + 8 * m:grad_at + 8 * m + 8, :]
    inverse = pivot(last, t_ref[HESS:HESS + 1, :], blocks)
    reduce_target(last, inverse, -t_ref[GRAD:GRAD + 1, :])
    for q in range(blocks - 1, -1, -1):
        for top in (8 * q + 4, 8 * q):
            some = range(top + 3, top - 1, -1)
            total = {(a, m): row(a, m) for a in some for m in range(q + 1)}
            for k in range(last, 8 * q + 7, -1):
                line = [row(k, m) for m in range(q + 1)]
                for a in some:
                    scale = u_ref[k, a:a + 1, :]
                    for m in range(q + 1):
                        total[a, m] = total[a, m] - scale * line[m]
            for (a, m), value in total.items():
                t_ref[first[a, m]:first[a, m] + 8, :] = value
        for a in range(8 * q + 7, 8 * q - 1, -1):
            total = [row(a, m) for m in range(q + 1)]
            for k in range(8 * q + 7, a, -1):
                scale = u_ref[k, a:a + 1, :]
                for m in range(q + 1):
                    total[m] = total[m] - scale * row(k, m)
            for m in range(q + 1):
                t_ref[first[a, m]:first[a, m] + 8, :] = total[m]
            at = first[a, q] + a % 8
            inverse = pivot(a, t_ref[at:at + 1, :], q + 1)
            reduce_target(a, inverse, t_ref[grad_at + a:grad_at + a + 1, :])
    c_ref[...] = jnp.zeros_like(c_ref)
    for q in range(blocks + 1):
        rows = range(8 * q, min(8 * q + 8, regress + 1))
        known = {}
        for k in rows:
            value = z_ref[k:k + 1, :]
            if q:
                products = u_ref[k, 0:8, :] * c_ref[0:8, :]
                for m in range(1, q):
                    products = products + u_ref[k, 8 * m:8 * m + 8, :] * c_ref[8 * m:8 * m + 8, :]
                value = value - jnp.sum(products, 0, keepdims=True)
            known[k] = value
        for k in rows:
            for b in range(8 * q, k):
                known[k] = known[k] - u_ref[k, b:b + 1, :] * known[b]
        for k in rows:
            c_ref[k:k + 1, :] = known[k]
    out_ref[...] = c_ref[...].T[:held]


def solve_call(regress, mine, other):
    held, lanes = mine.shape
    return pl.pallas_call(
        functools.partial(solve_kernel, regress),
        out_shape=jax.ShapeDtypeStruct((held, 128), F32),
        in_specs=[pl.BlockSpec(memory_space=pltpu.VMEM)] * 2,
        out_specs=pl.BlockSpec(memory_space=pltpu.VMEM),
        scratch_shapes=[
            pltpu.VMEM((lanes + 3 * regress, 128), F32),
            pltpu.VMEM((regress + 1, regress, 128), F32),
            pltpu.VMEM((72, 128), F32),
            pltpu.VMEM((128, 128), F32),
        ],
        compiler_params=pltpu.CompilerParams(vmem_limit_bytes=28 << 20),
    )(mine, other)


def apply_kernel(places, block, step, bits, *refs):
    part_refs = refs[:len(places)]
    hot_ref, feat_ref, hess_ref, grad_ref, coef_ref, next_ref, real_ref, own_ref = refs[len(places):]
    regress, rows = feat_ref.shape
    own = own_leaves(bits)
    for ref, owners in zip(part_refs, places):
        for at, place in enumerate(owners):
            value = ref[at * block:(at + 1) * block, :]
            own_ref[place * block:(place + 1) * block, :] = value
            real_ref[pl.ds(pl.multiple_of((place * block) ^ own, block), block), :] = value
    turned = own_ref[...].T[:80]
    high = turned.astype(BF16)
    both = jnp.concatenate([high, (turned - high.astype(F32)).astype(BF16)], 0)
    for start in range(0, rows, step):
        at = slice(start, start + step)
        picked = jnp.dot(both, hot_ref[:, at], preferred_element_type=F32)
        picked = picked[:80] + picked[80:]
        predicted = jnp.sum(picked[:regress] * feat_ref[:, at].astype(F32), 0, keepdims=True) + picked[regress:regress + 1]
        next_ref[:, at] = grad_ref[:, at] + hess_ref[:, at] * predicted
    coef_ref[...] = real_ref[...].T[:regress + 1]


def apply_call(places, block, parts, step, bits, hot, features, hessian, gradient):
    regress, rows = features.shape
    return pl.pallas_call(
        functools.partial(apply_kernel, places, block, step, bits),
        in_specs=[pl.BlockSpec(memory_space=pltpu.VMEM)] * (len(parts) + 4),
        out_specs=[pl.BlockSpec(memory_space=pltpu.VMEM)] * 2,
        out_shape=[jax.ShapeDtypeStruct((regress + 1, LEAVES), F32), jax.ShapeDtypeStruct((1, rows), F32)],
        scratch_shapes=[pltpu.VMEM((LEAVES, 128), F32), pltpu.VMEM((LEAVES, 128), F32)],
        compiler_params=pltpu.CompilerParams(vmem_limit_bytes=28 << 20),
    )(*parts, hot, features, hessian, gradient)


def combine_kernel(regress, plain, coded, size, starts, *refs):
    lanes = packed_lanes(regress)[2]
    pieces = len(starts)
    plain_refs, coded_refs, out_refs = refs[:plain * pieces], refs[plain * pieces:plain * pieces + coded], refs[plain * pieces + coded:]
    rows = plain_refs[0].shape[0]
    factors = [carried_factors(ref) for ref in coded_refs]

    def total(lane):
        piece = max(i for i in range(pieces) if starts[i] <= lane)
        at = lane - starts[piece]
        value = plain_refs[piece][:, at:at + 128]
        for p in range(1, plain):
            value = value + plain_refs[p * pieces + piece][:, at:at + 128]
        for ref, factor in zip(coded_refs, factors):
            value = value + decoded(regress, lane, ref, factor)
        return value

    head = total(0)
    hess_unit = jnp.clip(jnp.ceil(jnp.log2(head[:, HESS_ALL:HESS_ALL + 1] * (36.0 / 50000.0))), -100.0, 100.0)
    grad_unit = jnp.clip(jnp.ceil(jnp.log2(head[:, GRAD_ALL:GRAD_ALL + 1] * (6.0 / 50000.0))), -100.0, 100.0)
    own = [jnp.broadcast_to(jnp.exp2(-unit), (rows, 128)) for unit in (hess_unit, grad_unit)]
    for lane in range(0, lanes, 128):
        value = total(lane) if lane else head
        code = value * spread(regress, lane, *own)
        if lane == 0:
            at = lax.broadcasted_iota(I32, (rows, 128), 1)
            code = jnp.where(at == HESS_UNIT, hess_unit, jnp.where(at == GRAD_UNIT, grad_unit, code))
        if size:
            out_refs[1][:, lane:lane + 128] = value[:size]
        out_refs[0][:, lane:lane + 128] = code[size:]


def combine_call(regress, plain, coded, size):
    lanes = packed_lanes(regress)[2]
    rows = plain[0][0].shape[0]
    starts, at = [], 0
    for piece in plain[0]:
        starts.append(at)
        at += piece.shape[1]
    shapes = [jax.ShapeDtypeStruct((rows - size, lanes), F32)] + [jax.ShapeDtypeStruct((size, lanes), F32)] * (size > 0)
    operands = [piece for part in plain for piece in part] + [x.astype(F32) for x in coded]
    code, *own = pl.pallas_call(
        functools.partial(combine_kernel, regress, len(plain), len(coded), size, starts),
        in_specs=[pl.BlockSpec(memory_space=pltpu.VMEM)] * len(operands),
        out_specs=[pl.BlockSpec(memory_space=pltpu.VMEM)] * len(shapes),
        out_shape=shapes,
        compiler_params=pltpu.CompilerParams(vmem_limit_bytes=28 << 20),
    )(*operands)
    step = size or rows
    return [lax.optimization_barrier(code[at:at + step].astype(F16)) for at in range(0, rows - size, step)], own


def swap_rows(x, rows, distance):
    return lax.ppermute(x, "row", [(r, r ^ distance) for r in range(rows)])


def body(features, hessian, gradient, leaf_index, train_range):
    regress, local = features.shape
    rows = lax.axis_size("row")
    bits = rows.bit_length() - 1
    groups = row_groups(bits - 1)
    block = LEAVES >> bits
    subs = pair_layout(regress)[0]
    for kind in ("weight", "grad_high", "grad_low"):
        subs = subs + [(kind, 0, m) for m in range(regress // 16)]
    keeps, gots, shared = [], [], None
    for begin, end in CALLS:
        part = subs[16 * begin:16 * end]
        width = 256 * (end - begin)
        if shared is None:
            keep, send, *shared, hess_in, grad_in = first_call(part, width, FIRST_STEP, bits, train_range, features, hessian.reshape(1, local), gradient.reshape(1, local), leaf_index.reshape(1, local))
        else:
            keep, send = later_call(part, width, LATER_STEP, *shared[:2], hess_in, grad_in)
        keeps.append(keep)
        gots.append(lax.ppermute(send, "leaf", [(0, 1), (1, 0)]))
    plain, coded, size = [keeps, gots], [], LEAVES // 2
    for shift, count in groups:
        size >>= count
        sent, own = combine_call(regress, plain, coded, size)
        plain, coded = [own], [swap_rows(sent[d - 1], rows, d << shift) for d in sorted(range(1, 1 << count), key=(3, 1, 2).index)]
    (mine,), _ = combine_call(regress, plain, coded, 0)
    both = [mine, swap_rows(mine, rows, rows // 2)]
    both = [jnp.pad(x.astype(F32), ((0, -block % 8), (0, 0))) for x in both]
    coef = solve_call(regress, *both)[:block]
    both = jnp.concatenate([coef, lax.ppermute(coef, "leaf", [(0, 1), (1, 0)])], 0)
    held = [([0], both)]
    for shift, count in groups:
        names = [d for owners, _ in held for d in owners]
        array = jnp.concatenate([x for _, x in held], 0) if len(held) > 1 else held[0][1]
        held = held + [([n ^ (d << shift) for n in names], swap_rows(array, rows, d << shift)) for d in range(1, 1 << count)]
    places = [[place_of(bits, c, d) for d in owners for c in range(2)] for owners, _ in held]
    coefficients, following = apply_call(places, block, [x for _, x in held], APPLY_STEP, bits, *shared)
    return coefficients.T, following.reshape(local)


def solution(mesh):
    placed = (
        P(None, ("fold", "row", "leaf")),
        P(("fold", "row", "leaf")),
        P(("fold", "row", "leaf")),
        P(("fold", "row", "leaf"), None),
        P("fold"),
    )
    return jax.shard_map(
        body,
        mesh=mesh,
        in_specs=placed,
        out_specs=(P("fold", None), P(("fold", "row", "leaf"))),
        check_vma=False,
    )
```

```python
import functools
import jax
import jax.numpy as jnp
from jax import lax
from jax.experimental import pallas as pl
from jax.experimental.pallas import tpu as pltpu
from jax.sharding import PartitionSpec as P

LEAVES = 256
FIRST_STEP, LATER_STEP, APPLY_STEP = 4096, 8192, 4096
CALLS = ((0, 8), (8, 9))
HESS, GRAD, HESS_ALL, GRAD_ALL, HESS_UNIT, GRAD_UNIT = 28, 29, 30, 31, 60, 61
F32, BF16, F16, I32 = jnp.float32, jnp.bfloat16, jnp.float16, jnp.int32
NT = (((1,), (1,)), ((), ()))


def pair_layout(regress):
    subs, first, inner = [], {}, {}

    def mixed(q):
        for j in (0, 2):
            at = 16 * len(subs)
            first[8 * q + j, q], first[8 * q + j + 1, q] = at, at + 8
            inner[8 * q + 6 - j, q] = at + j + 1
            if j == 0:
                inner[8 * q + 5, q] = at + 10
            subs.append(("mixed", 8 * q, j))

    mixed(0)
    mixed(1)
    for q in range(0, regress // 8, 2):
        first[8 * q + 7, q], first[8 * q + 15, q + 1] = 16 * len(subs), 16 * len(subs) + 8
        subs.append(("ends", 8 * q, 0))
    for a in range(0, regress, 2):
        blocks = a // 8
        if a % 8 == 0 and blocks > 1:
            mixed(blocks)
        for one in (a, a + 1):
            for m in range(blocks // 2):
                first[one, 2 * m] = 16 * len(subs)
                first[one, 2 * m + 1] = 16 * len(subs) + 8
                subs.append(("full", one, m))
        if blocks % 2:
            first[a, blocks - 1] = 16 * len(subs)
            first[a + 1, blocks - 1] = 16 * len(subs) + 8
            subs.append(("half", a, blocks - 1))
    return subs, first, inner


def packed_lanes(regress):
    at = 16 * len(pair_layout(regress)[0])
    return at, at + regress, at + 3 * regress


def row_groups(bits):
    return [(shift, min(2, bits - shift)) for shift in range(0, bits, 2)]


def place_of(bits, core, row):
    place = core
    for shift, count in row_groups(bits - 1):
        place = (place << count) | ((row >> shift) & ((1 << count) - 1))
    return place


def own_leaves(bits):
    return place_of(bits, lax.axis_index("leaf"), lax.axis_index("row")) * (LEAVES >> bits)


def add_tiles(subs, out_width, step, feat_all, hess_all, grad_all, hot_all, keep_ref, send_ref, w_ref, before):
    regress, rows = feat_all.shape
    with_grad = subs[-1][0] == "grad_low"

    def chunk(k, fresh):
        at = pl.ds(k * step if isinstance(k, int) else pl.multiple_of(k * step, step), step)
        before(k, at)
        hess = hess_all[:, at]
        grad = grad_all[:, at].astype(BF16)
        hess_b = hess.astype(BF16)
        hot = hot_all[:, at]
        feat = feat_all[:, at]
        feat_f = feat.astype(F32)
        w_ref[...] = feat_f * hess

        @functools.lru_cache(None)
        def weight(a, count):
            return jnp.broadcast_to(w_ref[a:a + 1, :], (count, step))

        @functools.lru_cache(None)
        def weight_b(a):
            return weight(a, 16).astype(BF16)

        @functools.lru_cache(None)
        def twice(m):
            part = feat_f[8 * m:8 * m + 8]
            return jnp.concatenate([part, part], 0).astype(BF16)

        def eight(q, j, pair):
            part = feat_f[8 * q:8 * q + 8]
            value = weight(8 * q + j, 8) * part
            if not pair:
                return value
            moved = jnp.concatenate([part[7 - j:], part[:7 - j]], 0)
            return jnp.where(lax.broadcasted_iota(I32, (8, step), 0) <= j, value, weight(8 * q + 6 - j, 8) * moved)

        def join(one, other):
            return jnp.concatenate([one, other], 0).astype(BF16)

        def rows_of(sub):
            kind, a, m = sub
            if kind == "ends":
                return join(eight(a // 8, 7, False), eight(a // 8 + 1, 7, False))
            if kind == "mixed":
                tile = join(eight(a // 8, m, True), eight(a // 8, m + 1, m == 0))
                if a == 0 and m == 2:
                    row = 16 + lax.broadcasted_iota(I32, (16, step), 0)
                    tile_f = tile.astype(F32)
                    tile_f = jnp.where(row == HESS, hess_b.astype(F32), tile_f)
                    tile_f = jnp.where(row == GRAD, grad.astype(F32), tile_f)
                    tile = tile_f.astype(BF16)
                return tile
            if kind == "full":
                return weight_b(a) * feat[16 * m:16 * m + 16]
            if kind == "half":
                both = jnp.concatenate([weight(a, 8), weight(a + 1, 8)], 0).astype(BF16)
                return both * twice(m)
            if kind == "weight":
                return w_ref[16 * m:16 * m + 16, :].astype(BF16)
            exact = feat_f[16 * m:16 * m + 16] * grad.astype(F32)
            high = exact.astype(BF16)
            if kind == "grad_high":
                return high
            return (exact - high.astype(F32)).astype(BF16)

        for t in range(len(subs) * 16 // 256):
            tile = jnp.concatenate([rows_of(s) for s in subs[16 * t:16 * t + 16]], 0)
            part = lax.dot_general(hot, tile, NT, preferred_element_type=F32)
            if with_grad and (t + 1) * 256 == out_width:
                tail = part[:, 128:]
                part = jnp.concatenate([part[:, :128], tail + pltpu.roll(tail, 64, 1)], 1)
            lanes = slice(t * 256, t * 256 + 256)
            if fresh:
                keep_ref[:, lanes] = part[:LEAVES // 2]
                send_ref[:, lanes] = part[LEAVES // 2:]
            else:
                keep_ref[:, lanes] += part[:LEAVES // 2]
                send_ref[:, lanes] += part[LEAVES // 2:]

    chunk(0, True)
    if rows > step:
        lax.fori_loop(1, rows // step, lambda k, carry: (chunk(k, False), carry)[1], 0)


def first_kernel(subs, out_width, step, bits, range_hbm, feat_hbm, hess_hbm, grad_hbm, leaf_hbm, keep_ref, send_ref, hot_all, feat_all, hess_all, grad_all, hess_in, grad_in, leaf_all, range_ref, w_ref, total_ref, sems, feat_sems):
    rows = feat_all.shape[1]
    copies = [
        pltpu.make_async_copy(source, target, sems.at[i])
        for i, (source, target) in enumerate(((leaf_hbm, leaf_all), (range_hbm, range_ref), (hess_hbm, hess_all), (grad_hbm, grad_all)))
    ]

    def feat_copy(k):
        at = pl.ds(k * step if isinstance(k, int) else pl.multiple_of(k * step, step), step)
        return pltpu.make_async_copy(feat_hbm.at[:, at], feat_all.at[:, at], feat_sems.at[k])

    for copy in copies:
        copy.start()
    for k in range(rows // step):
        feat_copy(k).start()
    own = own_leaves(bits)
    names = lax.broadcasted_iota(I32, (LEAVES, 128), 0).astype(F32).astype(BF16)
    names = jnp.concatenate([names] * (step // 128), 1)
    copies[0].wait()
    for k in range(rows // step):
        at = slice(k * step, (k + 1) * step)
        leaf = (leaf_all[:, at] ^ own).astype(F32).astype(BF16)
        hot_all[:, at] = jnp.where(names == leaf, jnp.ones((), BF16), jnp.zeros((), BF16))
    for copy in copies[1:]:
        copy.wait()
    origin = (lax.axis_index("row") * 2 + lax.axis_index("leaf")) * rows
    position = origin + lax.broadcasted_iota(I32, (1, rows), 1)
    inside = jnp.where((position >= range_ref[0]) & (position < range_ref[1]), 1.0, 0.0)
    hess_in[...] = hess_all[...] * inside
    grad_in[...] = grad_all[...] * inside
    hess_total = jnp.sum(hess_in[...].astype(BF16).astype(F32), 1, keepdims=True)
    grad_total = jnp.sum(jnp.abs(grad_in[...].astype(BF16).astype(F32)), 1, keepdims=True)
    total_ref[0:1, :] = jnp.broadcast_to(hess_total, (1, 128))
    total_ref[1:2, :] = jnp.broadcast_to(grad_total, (1, 128))

    def before(k, at):
        feat_copy(k).wait()

    add_tiles(subs, out_width, step, feat_all, hess_in, grad_in, hot_all, keep_ref, send_ref, w_ref, before)
    lane = lax.broadcasted_iota(I32, (LEAVES // 2, 128), 1)
    for ref in (keep_ref, send_ref):
        first = jnp.where(lane == HESS_ALL, total_ref[0:1, :], ref[:, :128])
        ref[:, :128] = jnp.where(lane == GRAD_ALL, total_ref[1:2, :], first)


def later_kernel(subs, out_width, step, hot_all, feat_all, hess_in, grad_in, keep_ref, send_ref, w_ref):
    add_tiles(subs, out_width, step, feat_all, hess_in, grad_in, hot_all, keep_ref, send_ref, w_ref, lambda k, at: None)


def sums_cost(subs, out_width, rows):
    return pl.CostEstimate(flops=2 * LEAVES * rows * len(subs) * 16, bytes_accessed=rows * 656 + LEAVES * out_width * 4, transcendentals=0)


def first_call(subs, out_width, step, bits, train_range, features, hessian, gradient, leaf):
    regress, rows = features.shape
    return pl.pallas_call(
        functools.partial(first_kernel, subs, out_width, step, bits),
        in_specs=[pl.BlockSpec(memory_space=pltpu.HBM)] * 5,
        out_specs=[pl.BlockSpec(memory_space=pltpu.VMEM)] * 8,
        out_shape=[jax.ShapeDtypeStruct((LEAVES // 2, out_width), F32)] * 2
        + [jax.ShapeDtypeStruct((LEAVES, rows), BF16), jax.ShapeDtypeStruct((regress, rows), BF16)]
        + [jax.ShapeDtypeStruct((1, rows), F32)] * 4,
        scratch_shapes=[
            pltpu.VMEM((1, rows), I32),
            pltpu.SMEM((2,), I32),
            pltpu.VMEM((regress, step), F32),
            pltpu.VMEM((2, 128), F32),
            pltpu.SemaphoreType.DMA((4,)),
            pltpu.SemaphoreType.DMA((rows // step,)),
        ],
        compiler_params=pltpu.CompilerParams(vmem_limit_bytes=28 << 20),
        cost_estimate=sums_cost(subs, out_width, rows),
    )(*[pltpu.with_memory_space_constraint(x, pltpu.HBM) for x in (train_range, features, hessian, gradient, leaf)])


def later_call(subs, out_width, step, hot, features, hessian, gradient):
    regress, rows = features.shape
    return pl.pallas_call(
        functools.partial(later_kernel, subs, out_width, step),
        in_specs=[pl.BlockSpec(memory_space=pltpu.VMEM)] * 4,
        out_specs=[pl.BlockSpec(memory_space=pltpu.VMEM)] * 2,
        out_shape=[jax.ShapeDtypeStruct((LEAVES // 2, out_width), F32)] * 2,
        scratch_shapes=[pltpu.VMEM((regress, step), F32)],
        compiler_params=pltpu.CompilerParams(vmem_limit_bytes=28 << 20),
        cost_estimate=sums_cost(subs, out_width, rows),
    )(hot, features, hessian, gradient)


def spread(regress, lane, hess, grad):
    if lane >= packed_lanes(regress)[1]:
        return grad
    if lane:
        return hess
    at = lax.broadcasted_iota(I32, hess.shape, 1)
    return jnp.where((at == GRAD) | (at == GRAD_ALL), grad, hess)


def carried_factors(ref):
    wide = (ref.shape[0], 128)
    return [jnp.broadcast_to(jnp.exp2(ref[:, at:at + 1]), wide) for at in (HESS_UNIT, GRAD_UNIT)]


def decoded(regress, lane, ref, factors):
    return ref[:, lane:lane + 128] * spread(regress, lane, *factors)


def solve_kernel(regress, mine_ref, other_ref, out_ref, t_ref, u_ref, z_ref, c_ref):
    held, lanes = mine_ref.shape
    last_at, grad_at, _ = packed_lanes(regress)
    _, first, inner = pair_layout(regress)
    factors = [carried_factors(ref) for ref in (mine_ref, other_ref)]
    for lane in range(0, lanes, 128):
        tile = decoded(regress, lane, mine_ref, factors[0]) + decoded(regress, lane, other_ref, factors[1])
        tile = jnp.concatenate([tile, jnp.zeros((128 - held, 128), F32)], 0)
        t_ref[lane:lane + 128, :] = tile.T
    first = dict(first)
    for (a, m), at in inner.items():
        first[a, m] = lanes + 8 * list(inner).index((a, m))
        t_ref[first[a, m]:first[a, m] + 8, :] = t_ref[at:at + 8, :]
    last = regress
    for m in range(regress // 8):
        first[last, m] = last_at + 8 * m
    real = lax.broadcasted_iota(I32, (1, 128), 1) < held
    ridge = jnp.where(real, t_ref[HESS_ALL:HESS_ALL + 1, :] * (0.5 / LEAVES), 1.0)
    blocks = regress // 8

    def row(a, m):
        return t_ref[first[a, m]:first[a, m] + 8, :]

    def pivot(a, own, count):
        inverse = 1.0 / (own + ridge)
        for m in range(count):
            u_ref[a, 8 * m:8 * m + 8, :] = row(a, m) * inverse
        return inverse

    def reduce_target(a, inverse, value):
        scaled = value * inverse
        z_ref[a:a + 1, :] = scaled
        for m in range((a + 7) // 8):
            t_ref[grad_at + 8 * m:grad_at + 8 * m + 8, :] -= row(a, m) * scaled

    for m in range(blocks):
        t_ref[grad_at + 8 * m:grad_at + 8 * m + 8, :] = -t_ref[grad_at + 8 * m:grad_at + 8 * m + 8, :]
    inverse = pivot(last, t_ref[HESS:HESS + 1, :], blocks)
    reduce_target(last, inverse, -t_ref[GRAD:GRAD + 1, :])
    for q in range(blocks - 1, -1, -1):
        for top in (8 * q + 4, 8 * q):
            some = range(top + 3, top - 1, -1)
            total = {(a, m): row(a, m) for a in some for m in range(q + 1)}
            for k in range(last, 8 * q + 7, -1):
                line = [row(k, m) for m in range(q + 1)]
                for a in some:
                    scale = u_ref[k, a:a + 1, :]
                    for m in range(q + 1):
                        total[a, m] = total[a, m] - scale * line[m]
            for (a, m), value in total.items():
                t_ref[first[a, m]:first[a, m] + 8, :] = value
        for a in range(8 * q + 7, 8 * q - 1, -1):
            total = [row(a, m) for m in range(q + 1)]
            for k in range(8 * q + 7, a, -1):
                scale = u_ref[k, a:a + 1, :]
                for m in range(q + 1):
                    total[m] = total[m] - scale * row(k, m)
            for m in range(q + 1):
                t_ref[first[a, m]:first[a, m] + 8, :] = total[m]
            at = first[a, q] + a % 8
            inverse = pivot(a, t_ref[at:at + 1, :], q + 1)
            reduce_target(a, inverse, t_ref[grad_at + a:grad_at + a + 1, :])
    c_ref[...] = jnp.zeros_like(c_ref)
    for q in range(blocks + 1):
        rows = range(8 * q, min(8 * q + 8, regress + 1))
        known = {}
        for k in rows:
            value = z_ref[k:k + 1, :]
            if q:
                products = u_ref[k, 0:8, :] * c_ref[0:8, :]
                for m in range(1, q):
                    products = products + u_ref[k, 8 * m:8 * m + 8, :] * c_ref[8 * m:8 * m + 8, :]
                value = value - jnp.sum(products, 0, keepdims=True)
            known[k] = value
        for k in rows:
            for b in range(8 * q, k):
                known[k] = known[k] - u_ref[k, b:b + 1, :] * known[b]
        for k in rows:
            c_ref[k:k + 1, :] = known[k]
    out_ref[...] = c_ref[...].T[:held]


def solve_call(regress, mine, other):
    held, lanes = mine.shape
    return pl.pallas_call(
        functools.partial(solve_kernel, regress),
        out_shape=jax.ShapeDtypeStruct((held, 128), F32),
        in_specs=[pl.BlockSpec(memory_space=pltpu.VMEM)] * 2,
        out_specs=pl.BlockSpec(memory_space=pltpu.VMEM),
        scratch_shapes=[
            pltpu.VMEM((lanes + 3 * regress, 128), F32),
            pltpu.VMEM((regress + 1, regress, 128), F32),
            pltpu.VMEM((72, 128), F32),
            pltpu.VMEM((128, 128), F32),
        ],
        compiler_params=pltpu.CompilerParams(vmem_limit_bytes=28 << 20),
    )(mine, other)


def apply_kernel(places, block, step, bits, *refs):
    part_refs = refs[:len(places)]
    hot_ref, feat_ref, hess_ref, grad_ref, coef_ref, next_ref, real_ref, own_ref = refs[len(places):]
    regress, rows = feat_ref.shape
    own = own_leaves(bits)
    for ref, owners in zip(part_refs, places):
        for at, place in enumerate(owners):
            value = ref[at * block:(at + 1) * block, :]
            own_ref[place * block:(place + 1) * block, :] = value
            real_ref[pl.ds(pl.multiple_of((place * block) ^ own, block), block), :] = value
    turned = own_ref[...].T[:80]
    high = turned.astype(BF16)
    both = jnp.concatenate([high, (turned - high.astype(F32)).astype(BF16)], 0)
    for start in range(0, rows, step):
        at = slice(start, start + step)
        picked = jnp.dot(both, hot_ref[:, at], preferred_element_type=F32)
        picked = picked[:80] + picked[80:]
        predicted = jnp.sum(picked[:regress] * feat_ref[:, at].astype(F32), 0, keepdims=True) + picked[regress:regress + 1]
        next_ref[:, at] = grad_ref[:, at] + hess_ref[:, at] * predicted
    coef_ref[...] = real_ref[...].T[:regress + 1]


def apply_call(places, block, parts, step, bits, hot, features, hessian, gradient):
    regress, rows = features.shape
    return pl.pallas_call(
        functools.partial(apply_kernel, places, block, step, bits),
        in_specs=[pl.BlockSpec(memory_space=pltpu.VMEM)] * (len(parts) + 4),
        out_specs=[pl.BlockSpec(memory_space=pltpu.VMEM)] * 2,
        out_shape=[jax.ShapeDtypeStruct((regress + 1, LEAVES), F32), jax.ShapeDtypeStruct((1, rows), F32)],
        scratch_shapes=[pltpu.VMEM((LEAVES, 128), F32), pltpu.VMEM((LEAVES, 128), F32)],
        compiler_params=pltpu.CompilerParams(vmem_limit_bytes=28 << 20),
    )(*parts, hot, features, hessian, gradient)


def combine_kernel(regress, plain, coded, size, starts, *refs):
    lanes = packed_lanes(regress)[2]
    pieces = len(starts)
    plain_refs, coded_refs, out_refs = refs[:plain * pieces], refs[plain * pieces:plain * pieces + coded], refs[plain * pieces + coded:]
    rows = plain_refs[0].shape[0]
    factors = [carried_factors(ref) for ref in coded_refs]

    def total(lane):
        piece = max(i for i in range(pieces) if starts[i] <= lane)
        at = lane - starts[piece]
        value = plain_refs[piece][:, at:at + 128]
        for p in range(1, plain):
            value = value + plain_refs[p * pieces + piece][:, at:at + 128]
        for ref, factor in zip(coded_refs, factors):
            value = value + decoded(regress, lane, ref, factor)
        return value

    head = total(0)
    hess_unit = jnp.clip(jnp.ceil(jnp.log2(head[:, HESS_ALL:HESS_ALL + 1] * (36.0 / 50000.0))), -100.0, 100.0)
    grad_unit = jnp.clip(jnp.ceil(jnp.log2(head[:, GRAD_ALL:GRAD_ALL + 1] * (6.0 / 50000.0))), -100.0, 100.0)
    own = [jnp.broadcast_to(jnp.exp2(-unit), (rows, 128)) for unit in (hess_unit, grad_unit)]
    for lane in range(0, lanes, 128):
        value = total(lane) if lane else head
        code = value * spread(regress, lane, *own)
        if lane == 0:
            at = lax.broadcasted_iota(I32, (rows, 128), 1)
            code = jnp.where(at == HESS_UNIT, hess_unit, jnp.where(at == GRAD_UNIT, grad_unit, code))
        if size:
            out_refs[1][:, lane:lane + 128] = value[:size]
        out_refs[0][:, lane:lane + 128] = code[size:]


def combine_call(regress, plain, coded, size):
    lanes = packed_lanes(regress)[2]
    rows = plain[0][0].shape[0]
    starts, at = [], 0
    for piece in plain[0]:
        starts.append(at)
        at += piece.shape[1]
    shapes = [jax.ShapeDtypeStruct((rows - size, lanes), F32)] + [jax.ShapeDtypeStruct((size, lanes), F32)] * (size > 0)
    operands = [piece for part in plain for piece in part] + [x.astype(F32) for x in coded]
    code, *own = pl.pallas_call(
        functools.partial(combine_kernel, regress, len(plain), len(coded), size, starts),
        in_specs=[pl.BlockSpec(memory_space=pltpu.VMEM)] * len(operands),
        out_specs=[pl.BlockSpec(memory_space=pltpu.VMEM)] * len(shapes),
        out_shape=shapes,
        compiler_params=pltpu.CompilerParams(vmem_limit_bytes=28 << 20),
    )(*operands)
    step = size or rows
    return [lax.optimization_barrier(code[at:at + step].astype(F16)) for at in range(0, rows - size, step)], own


def swap_rows(x, rows, distance):
    return lax.ppermute(x, "row", [(r, r ^ distance) for r in range(rows)])


def body(features, hessian, gradient, leaf_index, train_range):
    regress, local = features.shape
    rows = lax.axis_size("row")
    bits = rows.bit_length() - 1
    groups = row_groups(bits - 1)
    block = LEAVES >> bits
    subs = pair_layout(regress)[0]
    for kind in ("weight", "grad_high", "grad_low"):
        subs = subs + [(kind, 0, m) for m in range(regress // 16)]
    keeps, gots, shared = [], [], None
    for begin, end in CALLS:
        part = subs[16 * begin:16 * end]
        width = 256 * (end - begin)
        if shared is None:
            keep, send, *shared, hess_in, grad_in = first_call(part, width, FIRST_STEP, bits, train_range, features, hessian.reshape(1, local), gradient.reshape(1, local), leaf_index.reshape(1, local))
        else:
            keep, send = later_call(part, width, LATER_STEP, *shared[:2], hess_in, grad_in)
        keeps.append(keep)
        gots.append(lax.ppermute(send, "leaf", [(0, 1), (1, 0)]))
    plain, coded, size = [keeps, gots], [], LEAVES // 2
    for shift, count in groups:
        size >>= count
        sent, own = combine_call(regress, plain, coded, size)
        plain, coded = [own], [swap_rows(sent[d - 1], rows, d << shift) for d in sorted(range(1, 1 << count), key=(3, 1, 2).index)]
    (mine,), _ = combine_call(regress, plain, coded, 0)
    both = [mine, swap_rows(mine, rows, rows // 2)]
    both = [jnp.pad(x.astype(F32), ((0, -block % 8), (0, 0))) for x in both]
    coef = solve_call(regress, *both)[:block]
    both = jnp.concatenate([coef, lax.ppermute(coef, "leaf", [(0, 1), (1, 0)])], 0)
    held = [([0], both)]
    for shift, count in groups:
        names = [d for owners, _ in held for d in owners]
        array = jnp.concatenate([x for _, x in held], 0) if len(held) > 1 else held[0][1]
        held = held + [([n ^ (d << shift) for n in names], swap_rows(array, rows, d << shift)) for d in range(1, 1 << count)]
    places = [[place_of(bits, c, d) for d in owners for c in range(2)] for owners, _ in held]
    coefficients, following = apply_call(places, block, [x for _, x in held], APPLY_STEP, bits, *shared)
    return coefficients.T, following.reshape(local)


def solution(mesh):
    placed = (
        P(None, ("fold", "row", "leaf")),
        P(("fold", "row", "leaf")),
        P(("fold", "row", "leaf")),
        P(("fold", "row", "leaf"), None),
        P("fold"),
    )
    return jax.shard_map(
        body,
        mesh=mesh,
        in_specs=placed,
        out_specs=(P("fold", None), P(("fold", "row", "leaf"))),
        check_vma=False,
    )
```

```python
import functools
import jax
import jax.numpy as jnp
from jax import lax
from jax.experimental import pallas as pl
from jax.experimental.pallas import tpu as pltpu
from jax.sharding import PartitionSpec as P

LEAVES = 256
FIRST_STEP, LATER_STEP, APPLY_STEP = 4096, 8192, 8192
CALLS = ((0, 8), (8, 9))
HESS, GRAD, HESS_ALL, GRAD_ALL, HESS_UNIT, GRAD_UNIT = 28, 29, 30, 31, 60, 61
F32, BF16, F16, I32 = jnp.float32, jnp.bfloat16, jnp.float16, jnp.int32
NT = (((1,), (1,)), ((), ()))


def pair_layout(regress):
    subs, first, inner = [], {}, {}

    def mixed(q):
        for j in (0, 2):
            at = 16 * len(subs)
            first[8 * q + j, q], first[8 * q + j + 1, q] = at, at + 8
            inner[8 * q + 6 - j, q] = at + j + 1
            if j == 0:
                inner[8 * q + 5, q] = at + 10
            subs.append(("mixed", 8 * q, j))

    mixed(0)
    mixed(1)
    for q in range(0, regress // 8, 2):
        first[8 * q + 7, q], first[8 * q + 15, q + 1] = 16 * len(subs), 16 * len(subs) + 8
        subs.append(("ends", 8 * q, 0))
    for a in range(0, regress, 2):
        blocks = a // 8
        if a % 8 == 0 and blocks > 1:
            mixed(blocks)
        for one in (a, a + 1):
            for m in range(blocks // 2):
                first[one, 2 * m] = 16 * len(subs)
                first[one, 2 * m + 1] = 16 * len(subs) + 8
                subs.append(("full", one, m))
        if blocks % 2:
            first[a, blocks - 1] = 16 * len(subs)
            first[a + 1, blocks - 1] = 16 * len(subs) + 8
            subs.append(("half", a, blocks - 1))
    return subs, first, inner


def packed_lanes(regress):
    at = 16 * len(pair_layout(regress)[0])
    return at, at + regress, at + 3 * regress


def row_groups(bits):
    return [(shift, min(2, bits - shift)) for shift in range(0, bits, 2)]


def place_of(bits, core, row):
    place = core
    for shift, count in row_groups(bits - 1):
        place = (place << count) | ((row >> shift) & ((1 << count) - 1))
    return place


def own_leaves(bits):
    return place_of(bits, lax.axis_index("leaf"), lax.axis_index("row")) * (LEAVES >> bits)


def add_tiles(subs, out_width, step, feat_all, hess_all, grad_all, hot_all, keep_ref, send_ref, w_ref, before):
    regress, rows = feat_all.shape
    with_grad = subs[-1][0] == "grad_low"

    def chunk(k, fresh):
        at = pl.ds(k * step if isinstance(k, int) else pl.multiple_of(k * step, step), step)
        before(k, at)
        hess = hess_all[:, at]
        grad = grad_all[:, at].astype(BF16)
        hess_b = hess.astype(BF16)
        hot = hot_all[:, at]
        feat = feat_all[:, at]
        feat_f = feat.astype(F32)
        w_ref[...] = feat_f * hess

        @functools.lru_cache(None)
        def weight(a, count):
            return jnp.broadcast_to(w_ref[a:a + 1, :], (count, step))

        @functools.lru_cache(None)
        def weight_b(a):
            return weight(a, 16).astype(BF16)

        @functools.lru_cache(None)
        def twice(m):
            part = feat_f[8 * m:8 * m + 8]
            return jnp.concatenate([part, part], 0).astype(BF16)

        def eight(q, j, pair):
            part = feat_f[8 * q:8 * q + 8]
            value = weight(8 * q + j, 8) * part
            if not pair:
                return value
            moved = jnp.concatenate([part[7 - j:], part[:7 - j]], 0)
            return jnp.where(lax.broadcasted_iota(I32, (8, step), 0) <= j, value, weight(8 * q + 6 - j, 8) * moved)

        def join(one, other):
            return jnp.concatenate([one, other], 0).astype(BF16)

        def rows_of(sub):
            kind, a, m = sub
            if kind == "ends":
                return join(eight(a // 8, 7, False), eight(a // 8 + 1, 7, False))
            if kind == "mixed":
                tile = join(eight(a // 8, m, True), eight(a // 8, m + 1, m == 0))
                if a == 0 and m == 2:
                    row = 16 + lax.broadcasted_iota(I32, (16, step), 0)
                    tile_f = tile.astype(F32)
                    tile_f = jnp.where(row == HESS, hess_b.astype(F32), tile_f)
                    tile_f = jnp.where(row == GRAD, grad.astype(F32), tile_f)
                    tile = tile_f.astype(BF16)
                return tile
            if kind == "full":
                return weight_b(a) * feat[16 * m:16 * m + 16]
            if kind == "half":
                both = jnp.concatenate([weight(a, 8), weight(a + 1, 8)], 0).astype(BF16)
                return both * twice(m)
            if kind == "weight":
                return w_ref[16 * m:16 * m + 16, :].astype(BF16)
            exact = feat_f[16 * m:16 * m + 16] * grad.astype(F32)
            high = exact.astype(BF16)
            if kind == "grad_high":
                return high
            return (exact - high.astype(F32)).astype(BF16)

        for t in range(len(subs) * 16 // 256):
            tile = jnp.concatenate([rows_of(s) for s in subs[16 * t:16 * t + 16]], 0)
            part = lax.dot_general(hot, tile, NT, preferred_element_type=F32)
            if with_grad and (t + 1) * 256 == out_width:
                tail = part[:, 128:]
                part = jnp.concatenate([part[:, :128], tail + pltpu.roll(tail, 64, 1)], 1)
            lanes = slice(t * 256, t * 256 + 256)
            if fresh:
                keep_ref[:, lanes] = part[:LEAVES // 2]
                send_ref[:, lanes] = part[LEAVES // 2:]
            else:
                keep_ref[:, lanes] += part[:LEAVES // 2]
                send_ref[:, lanes] += part[LEAVES // 2:]

    chunk(0, True)
    if rows > step:
        lax.fori_loop(1, rows // step, lambda k, carry: (chunk(k, False), carry)[1], 0)


def first_kernel(subs, out_width, step, bits, range_hbm, feat_hbm, hess_hbm, grad_hbm, leaf_hbm, keep_ref, send_ref, hot_all, feat_all, hess_all, grad_all, hess_in, grad_in, leaf_all, range_ref, w_ref, total_ref, sems, feat_sems):
    rows = feat_all.shape[1]
    copies = [
        pltpu.make_async_copy(source, target, sems.at[i])
        for i, (source, target) in enumerate(((leaf_hbm, leaf_all), (range_hbm, range_ref), (hess_hbm, hess_all), (grad_hbm, grad_all)))
    ]

    def feat_copy(k):
        at = pl.ds(k * step if isinstance(k, int) else pl.multiple_of(k * step, step), step)
        return pltpu.make_async_copy(feat_hbm.at[:, at], feat_all.at[:, at], feat_sems.at[k])

    for copy in copies:
        copy.start()
    for k in range(rows // step):
        feat_copy(k).start()
    own = own_leaves(bits)
    names = lax.broadcasted_iota(I32, (LEAVES, 128), 0).astype(F32).astype(BF16)
    names = jnp.concatenate([names] * (step // 128), 1)
    copies[0].wait()
    for k in range(rows // step):
        at = slice(k * step, (k + 1) * step)
        leaf = (leaf_all[:, at] ^ own).astype(F32).astype(BF16)
        hot_all[:, at] = jnp.where(names == leaf, jnp.ones((), BF16), jnp.zeros((), BF16))
    for copy in copies[1:]:
        copy.wait()
    origin = (lax.axis_index("row") * 2 + lax.axis_index("leaf")) * rows
    position = origin + lax.broadcasted_iota(I32, (1, rows), 1)
    inside = jnp.where((position >= range_ref[0]) & (position < range_ref[1]), 1.0, 0.0)
    hess_in[...] = hess_all[...] * inside
    grad_in[...] = grad_all[...] * inside
    hess_total = jnp.sum(hess_in[...].astype(BF16).astype(F32), 1, keepdims=True)
    grad_total = jnp.sum(jnp.abs(grad_in[...].astype(BF16).astype(F32)), 1, keepdims=True)
    total_ref[0:1, :] = jnp.broadcast_to(hess_total, (1, 128))
    total_ref[1:2, :] = jnp.broadcast_to(grad_total, (1, 128))

    def before(k, at):
        feat_copy(k).wait()

    add_tiles(subs, out_width, step, feat_all, hess_in, grad_in, hot_all, keep_ref, send_ref, w_ref, before)
    lane = lax.broadcasted_iota(I32, (LEAVES // 2, 128), 1)
    for ref in (keep_ref, send_ref):
        first = jnp.where(lane == HESS_ALL, total_ref[0:1, :], ref[:, :128])
        ref[:, :128] = jnp.where(lane == GRAD_ALL, total_ref[1:2, :], first)


def later_kernel(subs, out_width, step, hot_all, feat_all, hess_in, grad_in, keep_ref, send_ref, w_ref):
    add_tiles(subs, out_width, step, feat_all, hess_in, grad_in, hot_all, keep_ref, send_ref, w_ref, lambda k, at: None)


def sums_cost(subs, out_width, rows):
    return pl.CostEstimate(flops=2 * LEAVES * rows * len(subs) * 16, bytes_accessed=rows * 656 + LEAVES * out_width * 4, transcendentals=0)


def first_call(subs, out_width, step, bits, train_range, features, hessian, gradient, leaf):
    regress, rows = features.shape
    return pl.pallas_call(
        functools.partial(first_kernel, subs, out_width, step, bits),
        in_specs=[pl.BlockSpec(memory_space=pltpu.HBM)] * 5,
        out_specs=[pl.BlockSpec(memory_space=pltpu.VMEM)] * 8,
        out_shape=[jax.ShapeDtypeStruct((LEAVES // 2, out_width), F32)] * 2
        + [jax.ShapeDtypeStruct((LEAVES, rows), BF16), jax.ShapeDtypeStruct((regress, rows), BF16)]
        + [jax.ShapeDtypeStruct((1, rows), F32)] * 4,
        scratch_shapes=[
            pltpu.VMEM((1, rows), I32),
            pltpu.SMEM((2,), I32),
            pltpu.VMEM((regress, step), F32),
            pltpu.VMEM((2, 128), F32),
            pltpu.SemaphoreType.DMA((4,)),
            pltpu.SemaphoreType.DMA((rows // step,)),
        ],
        compiler_params=pltpu.CompilerParams(vmem_limit_bytes=28 << 20),
        cost_estimate=sums_cost(subs, out_width, rows),
    )(*[pltpu.with_memory_space_constraint(x, pltpu.HBM) for x in (train_range, features, hessian, gradient, leaf)])


def later_call(subs, out_width, step, hot, features, hessian, gradient):
    regress, rows = features.shape
    return pl.pallas_call(
        functools.partial(later_kernel, subs, out_width, step),
        in_specs=[pl.BlockSpec(memory_space=pltpu.VMEM)] * 4,
        out_specs=[pl.BlockSpec(memory_space=pltpu.VMEM)] * 2,
        out_shape=[jax.ShapeDtypeStruct((LEAVES // 2, out_width), F32)] * 2,
        scratch_shapes=[pltpu.VMEM((regress, step), F32)],
        compiler_params=pltpu.CompilerParams(vmem_limit_bytes=28 << 20),
        cost_estimate=sums_cost(subs, out_width, rows),
    )(hot, features, hessian, gradient)


def spread(regress, lane, hess, grad):
    if lane >= packed_lanes(regress)[1]:
        return grad
    if lane:
        return hess
    at = lax.broadcasted_iota(I32, hess.shape, 1)
    return jnp.where((at == GRAD) | (at == GRAD_ALL), grad, hess)


def carried_factors(ref):
    wide = (ref.shape[0], 128)
    return [jnp.broadcast_to(jnp.exp2(ref[:, at:at + 1]), wide) for at in (HESS_UNIT, GRAD_UNIT)]


def decoded(regress, lane, ref, factors):
    return ref[:, lane:lane + 128] * spread(regress, lane, *factors)


def solve_kernel(regress, mine_ref, other_ref, out_ref, t_ref, u_ref, z_ref, c_ref):
    held, lanes = mine_ref.shape
    last_at, grad_at, _ = packed_lanes(regress)
    _, first, inner = pair_layout(regress)
    factors = [carried_factors(ref) for ref in (mine_ref, other_ref)]
    for lane in range(0, lanes, 128):
        tile = decoded(regress, lane, mine_ref, factors[0]) + decoded(regress, lane, other_ref, factors[1])
        tile = jnp.concatenate([tile, jnp.zeros((128 - held, 128), F32)], 0)
        t_ref[lane:lane + 128, :] = tile.T
    first = dict(first)
    for (a, m), at in inner.items():
        first[a, m] = lanes + 8 * list(inner).index((a, m))
        t_ref[first[a, m]:first[a, m] + 8, :] = t_ref[at:at + 8, :]
    last = regress
    for m in range(regress // 8):
        first[last, m] = last_at + 8 * m
    real = lax.broadcasted_iota(I32, (1, 128), 1) < held
    ridge = jnp.where(real, t_ref[HESS_ALL:HESS_ALL + 1, :] * (0.5 / LEAVES), 1.0)
    blocks = regress // 8

    def row(a, m):
        return t_ref[first[a, m]:first[a, m] + 8, :]

    def pivot(a, own, count):
        inverse = 1.0 / (own + ridge)
        for m in range(count):
            u_ref[a, 8 * m:8 * m + 8, :] = row(a, m) * inverse
        return inverse

    def reduce_target(a, inverse, value):
        scaled = value * inverse
        z_ref[a:a + 1, :] = scaled
        for m in range((a + 7) // 8):
            t_ref[grad_at + 8 * m:grad_at + 8 * m + 8, :] -= row(a, m) * scaled

    for m in range(blocks):
        t_ref[grad_at + 8 * m:grad_at + 8 * m + 8, :] = -t_ref[grad_at + 8 * m:grad_at + 8 * m + 8, :]
    inverse = pivot(last, t_ref[HESS:HESS + 1, :], blocks)
    reduce_target(last, inverse, -t_ref[GRAD:GRAD + 1, :])
    for q in range(blocks - 1, -1, -1):
        for top in (8 * q + 4, 8 * q):
            some = range(top + 3, top - 1, -1)
            total = {(a, m): row(a, m) for a in some for m in range(q + 1)}
            for k in range(last, 8 * q + 7, -1):
                line = [row(k, m) for m in range(q + 1)]
                for a in some:
                    scale = u_ref[k, a:a + 1, :]
                    for m in range(q + 1):
                        total[a, m] = total[a, m] - scale * line[m]
            for (a, m), value in total.items():
                t_ref[first[a, m]:first[a, m] + 8, :] = value
        for a in range(8 * q + 7, 8 * q - 1, -1):
            total = [row(a, m) for m in range(q + 1)]
            for k in range(8 * q + 7, a, -1):
                scale = u_ref[k, a:a + 1, :]
                for m in range(q + 1):
                    total[m] = total[m] - scale * row(k, m)
            for m in range(q + 1):
                t_ref[first[a, m]:first[a, m] + 8, :] = total[m]
            at = first[a, q] + a % 8
            inverse = pivot(a, t_ref[at:at + 1, :], q + 1)
            reduce_target(a, inverse, t_ref[grad_at + a:grad_at + a + 1, :])
    c_ref[...] = jnp.zeros_like(c_ref)
    for q in range(blocks + 1):
        rows = range(8 * q, min(8 * q + 8, regress + 1))
        known = {}
        for k in rows:
            value = z_ref[k:k + 1, :]
            if q:
                products = u_ref[k, 0:8, :] * c_ref[0:8, :]
                for m in range(1, q):
                    products = products + u_ref[k, 8 * m:8 * m + 8, :] * c_ref[8 * m:8 * m + 8, :]
                value = value - jnp.sum(products, 0, keepdims=True)
            known[k] = value
        for k in rows:
            for b in range(8 * q, k):
                known[k] = known[k] - u_ref[k, b:b + 1, :] * known[b]
        for k in rows:
            c_ref[k:k + 1, :] = known[k]
    out_ref[...] = c_ref[...].T[:held]


def solve_call(regress, mine, other):
    held, lanes = mine.shape
    return pl.pallas_call(
        functools.partial(solve_kernel, regress),
        out_shape=jax.ShapeDtypeStruct((held, 128), F32),
        in_specs=[pl.BlockSpec(memory_space=pltpu.VMEM)] * 2,
        out_specs=pl.BlockSpec(memory_space=pltpu.VMEM),
        scratch_shapes=[
            pltpu.VMEM((lanes + 3 * regress, 128), F32),
            pltpu.VMEM((regress + 1, regress, 128), F32),
            pltpu.VMEM((72, 128), F32),
            pltpu.VMEM((128, 128), F32),
        ],
        compiler_params=pltpu.CompilerParams(vmem_limit_bytes=28 << 20),
    )(mine, other)


def apply_kernel(places, block, step, bits, *refs):
    part_refs = refs[:len(places)]
    hot_ref, feat_ref, hess_ref, grad_ref, coef_ref, next_ref, real_ref, own_ref = refs[len(places):]
    regress, rows = feat_ref.shape
    own = own_leaves(bits)
    for ref, owners in zip(part_refs, places):
        for at, place in enumerate(owners):
            value = ref[at * block:(at + 1) * block, :]
            own_ref[place * block:(place + 1) * block, :] = value
            real_ref[pl.ds(pl.multiple_of((place * block) ^ own, block), block), :] = value
    turned = own_ref[...].T[:80]
    high = turned.astype(BF16)
    both = jnp.concatenate([high, (turned - high.astype(F32)).astype(BF16)], 0)
    for start in range(0, rows, step):
        at = slice(start, start + step)
        picked = jnp.dot(both, hot_ref[:, at], preferred_element_type=F32)
        picked = picked[:80] + picked[80:]
        predicted = jnp.sum(picked[:regress] * feat_ref[:, at].astype(F32), 0, keepdims=True) + picked[regress:regress + 1]
        next_ref[:, at] = grad_ref[:, at] + hess_ref[:, at] * predicted
    coef_ref[...] = real_ref[...].T[:regress + 1]


def apply_call(places, block, parts, step, bits, hot, features, hessian, gradient):
    regress, rows = features.shape
    return pl.pallas_call(
        functools.partial(apply_kernel, places, block, step, bits),
        in_specs=[pl.BlockSpec(memory_space=pltpu.VMEM)] * (len(parts) + 4),
        out_specs=[pl.BlockSpec(memory_space=pltpu.VMEM)] * 2,
        out_shape=[jax.ShapeDtypeStruct((regress + 1, LEAVES), F32), jax.ShapeDtypeStruct((1, rows), F32)],
        scratch_shapes=[pltpu.VMEM((LEAVES, 128), F32), pltpu.VMEM((LEAVES, 128), F32)],
        compiler_params=pltpu.CompilerParams(vmem_limit_bytes=28 << 20),
    )(*parts, hot, features, hessian, gradient)


def combine_kernel(regress, plain, coded, size, starts, *refs):
    lanes = packed_lanes(regress)[2]
    pieces = len(starts)
    plain_refs, coded_refs, out_refs = refs[:plain * pieces], refs[plain * pieces:plain * pieces + coded], refs[plain * pieces + coded:]
    rows = plain_refs[0].shape[0]
    factors = [carried_factors(ref) for ref in coded_refs]

    def total(lane):
        piece = max(i for i in range(pieces) if starts[i] <= lane)
        at = lane - starts[piece]
        value = plain_refs[piece][:, at:at + 128]
        for p in range(1, plain):
            value = value + plain_refs[p * pieces + piece][:, at:at + 128]
        for ref, factor in zip(coded_refs, factors):
            value = value + decoded(regress, lane, ref, factor)
        return value

    head = total(0)
    hess_unit = jnp.clip(jnp.ceil(jnp.log2(head[:, HESS_ALL:HESS_ALL + 1] * (36.0 / 50000.0))), -125.0, 125.0)
    grad_unit = jnp.clip(jnp.ceil(jnp.log2(head[:, GRAD_ALL:GRAD_ALL + 1] * (6.0 / 50000.0))), -125.0, 125.0)
    own = [jnp.broadcast_to(jnp.exp2(-unit), (rows, 128)) for unit in (hess_unit, grad_unit)]
    for lane in range(0, lanes, 128):
        value = total(lane) if lane else head
        code = value * spread(regress, lane, *own)
        if lane == 0:
            at = lax.broadcasted_iota(I32, (rows, 128), 1)
            code = jnp.where(at == HESS_UNIT, hess_unit, jnp.where(at == GRAD_UNIT, grad_unit, code))
        if size:
            out_refs[1][:, lane:lane + 128] = value[:size]
        out_refs[0][:, lane:lane + 128] = code[size:]


def combine_call(regress, plain, coded, size):
    lanes = packed_lanes(regress)[2]
    rows = plain[0][0].shape[0]
    starts, at = [], 0
    for piece in plain[0]:
        starts.append(at)
        at += piece.shape[1]
    shapes = [jax.ShapeDtypeStruct((rows - size, lanes), F32)] + [jax.ShapeDtypeStruct((size, lanes), F32)] * (size > 0)
    operands = [piece for part in plain for piece in part] + [x.astype(F32) for x in coded]
    code, *own = pl.pallas_call(
        functools.partial(combine_kernel, regress, len(plain), len(coded), size, starts),
        in_specs=[pl.BlockSpec(memory_space=pltpu.VMEM)] * len(operands),
        out_specs=[pl.BlockSpec(memory_space=pltpu.VMEM)] * len(shapes),
        out_shape=shapes,
        compiler_params=pltpu.CompilerParams(vmem_limit_bytes=28 << 20),
    )(*operands)
    step = size or rows
    return [lax.optimization_barrier(code[at:at + step].astype(F16)) for at in range(0, rows - size, step)], own


def swap_rows(x, rows, distance):
    return lax.ppermute(x, "row", [(r, r ^ distance) for r in range(rows)])


def body(features, hessian, gradient, leaf_index, train_range):
    regress, local = features.shape
    rows = lax.axis_size("row")
    bits = rows.bit_length() - 1
    groups = row_groups(bits - 1)
    block = LEAVES >> bits
    subs = pair_layout(regress)[0]
    for kind in ("weight", "grad_high", "grad_low"):
        subs = subs + [(kind, 0, m) for m in range(regress // 16)]
    keeps, gots, shared = [], [], None
    for begin, end in CALLS:
        part = subs[16 * begin:16 * end]
        width = 256 * (end - begin)
        if shared is None:
            keep, send, *shared, hess_in, grad_in = first_call(part, width, FIRST_STEP, bits, train_range, features, hessian.reshape(1, local), gradient.reshape(1, local), leaf_index.reshape(1, local))
        else:
            keep, send = later_call(part, width, LATER_STEP, *shared[:2], hess_in, grad_in)
        keeps.append(keep)
        gots.append(lax.ppermute(send, "leaf", [(0, 1), (1, 0)]))
    plain, coded, size = [keeps, gots], [], LEAVES // 2
    for shift, count in groups:
        size >>= count
        sent, own = combine_call(regress, plain, coded, size)
        plain, coded = [own], [swap_rows(sent[d - 1], rows, d << shift) for d in sorted(range(1, 1 << count), key=(3, 1, 2).index)]
    (mine,), _ = combine_call(regress, plain, coded, 0)
    both = [mine, swap_rows(mine, rows, rows // 2)]
    both = [jnp.pad(x.astype(F32), ((0, -block % 8), (0, 0))) for x in both]
    coef = solve_call(regress, *both)[:block]
    both = jnp.concatenate([coef, lax.ppermute(coef, "leaf", [(0, 1), (1, 0)])], 0)
    held = [([0], both)]
    for shift, count in groups:
        names = [d for owners, _ in held for d in owners]
        array = jnp.concatenate([x for _, x in held], 0) if len(held) > 1 else held[0][1]
        held = held + [([n ^ (d << shift) for n in names], swap_rows(array, rows, d << shift)) for d in range(1, 1 << count)]
    places = [[place_of(bits, c, d) for d in owners for c in range(2)] for owners, _ in held]
    coefficients, following = apply_call(places, block, [x for _, x in held], APPLY_STEP, bits, *shared)
    return coefficients.T, following.reshape(local)


def solution(mesh):
    placed = (
        P(None, ("fold", "row", "leaf")),
        P(("fold", "row", "leaf")),
        P(("fold", "row", "leaf")),
        P(("fold", "row", "leaf"), None),
        P("fold"),
    )
    return jax.shard_map(
        body,
        mesh=mesh,
        in_specs=placed,
        out_specs=(P("fold", None), P(("fold", "row", "leaf"))),
        check_vma=False,
    )
```
